128 devices in a mesh: heads: 4 (over x), ctx: 32 (over y, z, core).
Axes of the slice: x: 4, y: 4, z: 4, core: 2. Of those that a mesh axis runs over, the one named last changes fastest.
Arguments:
- queries: bfloat16 [32, 128, 192], P('ctx', 'heads')
- latent_store_cache: bfloat16 [8, 49152, 576], P(None, 'ctx')
- new_latent: bfloat16 [32, 576], replicated
- cache_lengths: int32 [8], replicated, may hold values from 1 to 49152, 196608 in all
- key_up: bfloat16 [128, 128, 512], P('heads'), may hold values from -0.5 to 0.5
- value_up: bfloat16 [128, 512, 128], P('heads'), may hold values from -0.25 to 0.25
- out_proj: bfloat16 [16384, 7168], P('heads', 'ctx'), may hold values from -0.046875 to 0.046875
Outputs:
- attention_result: bfloat16 [32, 7168], P(None, 'ctx')
The draws below stay inside these ranges and needn't reach their ends.
Inputs may be any that keep to these rules, and one draw needn't show every extreme that they name: Request b has cache_lengths[b] valid positions at the start of its cache; some request has exactly 49152.
All inputs are finite; a program needn't handle non-finite values.
Results may differ from the reference program's by a relative error of at most 0.023.
Values may be sent and summed in bfloat16 or wider, within the bound.
A program may use at most 320 MiB of HBM per device.

```python
import math
import jax
import jax.numpy as jnp
import numpy as np
from jax import lax

D = 7168
H = 128
NOPE = 128
ROPE = 64
LATENT = 512
VDIM = 128
REQS = 8
STEPS = 4
CACHE = 49152
ROWS = 32


def draw_queries(key, part):
    key = jax.random.fold_in(key, 11)
    first = jax.random.fold_in(key, 0)
    shape = (ROWS, H, NOPE + ROPE)
    base = jax.random.truncated_normal(first, -6.0, 6.0, shape, jnp.float32)
    return base.astype(jnp.bfloat16)


def draw_latent_store_cache(key, part):
    key = jax.random.fold_in(key, 12)
    shape = (REQS, CACHE, LATENT + ROPE)
    base = jax.random.truncated_normal(key, -6.0, 6.0, shape, jnp.float32)
    return base.astype(jnp.bfloat16)


def draw_new_latent(key, part):
    key = jax.random.fold_in(key, 13)
    shape = (ROWS, LATENT + ROPE)
    base = jax.random.truncated_normal(key, -6.0, 6.0, shape, jnp.float32)
    return base.astype(jnp.bfloat16)


def shard_levels(stream_key, extent, shards, smallest, top_value):
    factor_of = 1.0
    for dim, blocks in shards:
        heights = jax.random.uniform(jax.random.fold_in(jax.random.fold_in(stream_key, 6), dim), (blocks,), jnp.float32, smallest / len(shards), top_value / len(shards))
        factor_of = factor_of * jnp.repeat(jnp.exp(heights), extent[dim] // blocks).reshape((-1,) + (1,) * (len(extent) - 1 - dim))
    return factor_of


def profile(number_of, total, limit, lean):
    loads = [(1 << 20) // math.isqrt(rank ** lean) + 1 for rank in range(2, number_of + 1)]
    surplus, holding = total - limit - (number_of - 1), [1] * (number_of - 1)
    while surplus > 0:
        candidates = [i for i in range(number_of - 1) if holding[i] < limit]
        whole, budget = sum([loads[i] for i in candidates]), surplus
        for i in candidates:
            more = min(limit - holding[i], max(1, budget * loads[i] // whole), surplus)
            holding[i] = holding[i] + more
            surplus = surplus - more
    return np.array([limit] + holding)


def ragged(key, count, total, limit, lean):
    if count == 2:
        one = jax.random.randint(key, (), max(1, total - limit), min(limit, total - 1) + 1)
        return jnp.stack([one, total - one])
    tallies = jnp.asarray(profile(count, total, limit, lean), jnp.int32)
    twos = (count - 1) // 2
    source_of, receiver = tallies[1:1 + 2 * twos:2], tallies[2:2 + 2 * twos:2]
    room = jnp.minimum(source_of - 1, limit - receiver)
    passed = jax.random.randint(jax.random.fold_in(key, 1), (twos,), 0, 1 << 20) % (room + 1)
    tallies = tallies.at[1:1 + 2 * twos:2].set(source_of - passed).at[2:2 + 2 * twos:2].set(receiver + passed)
    return tallies[jax.random.permutation(jax.random.fold_in(key, 2), count)]


def gaussian(key, shape, deviation, limit, cuts=(), held_as=jnp.bfloat16):
    result = jax.random.normal(key, shape, jnp.float32) * deviation
    if len(cuts) > 0:
        result = shard_levels(key, shape, cuts, -0.22, 0.18) * result
    return jnp.clip(result, min=-limit, max=limit).astype(held_as)


def setup_inputs(seed: int = 0) -> dict:
    key_list = jax.random.split(jax.random.key(seed), 8)
    return {
        "queries": draw_queries(jax.random.fold_in(key_list[7], 71), 0),
        "latent_store_cache": draw_latent_store_cache(jax.random.fold_in(key_list[7], 71), 0),
        "new_latent": draw_new_latent(jax.random.fold_in(key_list[7], 71), 0),
        "cache_lengths": ragged(key_list[3], REQS, REQS * CACHE // 2, CACHE, 1).astype(jnp.int32),
        "key_up": gaussian(key_list[4], (H, NOPE, LATENT), NOPE ** -0.5, 0.5, ((0, 4),)),
        "value_up": gaussian(key_list[5], (H, LATENT, VDIM), LATENT ** -0.5, 0.25, ((0, 4),)),
        "out_proj": gaussian(key_list[6], (H * VDIM, D), (H * VDIM) ** -0.5, 0.046875, ((0, 4), (1, 32))),
    }


NEG = -1e+30

def reference(queries, latent_store_cache, new_latent, cache_lengths, key_up, value_up, out_proj):
    q_lat = jnp.einsum('rhd,hdc->rhc', queries[:, :, :NOPE].astype(jnp.float32), key_up.astype(jnp.float32)).astype(jnp.bfloat16)
    q_full = jnp.concatenate([q_lat, queries[:, :, NOPE:]], axis=2)
    q_req = q_full.reshape(REQS, STEPS, H, LATENT + ROPE)
    fresh = new_latent.reshape(REQS, STEPS, LATENT + ROPE)
    scale = 1.0 / jnp.sqrt(jnp.float32(NOPE + ROPE))

    def one_request(items):
        query_block, cache_block, fresh_block, cache_length_value = items
        keys = jnp.concatenate([cache_block, fresh_block], axis=0).astype(jnp.float32)
        score = jnp.einsum('thc,kc->thk', query_block.astype(jnp.float32), keys) * scale
        position = jnp.arange(CACHE + STEPS, dtype=jnp.int32)
        step_ids = jnp.arange(STEPS, dtype=jnp.int32)
        in_cache = (position < cache_length_value)[None, :]
        in_fresh = (position[None, :] >= CACHE) & (position[None, :] - CACHE <= step_ids[:, None])
        valid = (in_cache | in_fresh)[:, None, :]
        masked = jnp.where(valid, score, NEG)
        top = lax.optimization_barrier(jnp.max(masked, axis=2, keepdims=True))
        weight = jnp.where(valid, jnp.exp(masked - top), 0.0)
        total = lax.optimization_barrier(jnp.sum(weight, axis=2))
        weight_b = weight.astype(jnp.bfloat16).astype(jnp.float32)
        summed = jnp.einsum('thk,kc->thc', weight_b, keys[:, :LATENT])
        return summed / total[:, :, None]
    o_lat = lax.map(one_request, (q_req, latent_store_cache, fresh, cache_lengths))
    o_lat = o_lat.reshape(ROWS, H, LATENT)
    head_out = jnp.einsum('rhc,hcv->rhv', o_lat, value_up.astype(jnp.float32), precision=lax.Precision.HIGHEST).astype(jnp.bfloat16)
    head_out = head_out.reshape(ROWS, H * VDIM)
    return jnp.dot(head_out, out_proj, preferred_element_type=jnp.float32).astype(jnp.bfloat16)
```

```python
import functools
import math

import jax
import jax.numpy as jnp
from jax import lax
from jax.experimental import pallas as pl
from jax.experimental.pallas import tpu as pltpu
from jax.sharding import PartitionSpec as P

NEG = -3e38
MESH = pl.DeviceIdType.MESH
F32 = jnp.float32
BF16 = jnp.bfloat16


def kernel(
    n,
    groups,
    reqs,
    queries,
    cache,
    fresh,
    lengths,
    key_up,
    value_up,
    out_proj,
    out,
    kc,
    ku,
    vu,
    op,
    nl,
    qg,
    qn,
    qrope,
    ql,
    qfull,
    osum,
    stat,
    sbuf,
    sstat,
    rbuf,
    rstat,
    ho,
    hg,
    xb,
    cache_sem,
    local_sem,
    q_send,
    q_recv,
    p_send,
    p_recv,
    t_send,
    t_recv,
    h_send,
    h_recv,
    x_send,
    x_recv,
):
    me = lax.axis_index("ctx")
    group = lax.axis_index("heads")
    rows = n
    heads = key_up.shape[0]
    nope = key_up.shape[1]
    latent = key_up.shape[2]
    chunks = latent // 128
    width = cache.shape[2]
    keys = cache.shape[1]
    steps = rows // reqs
    per = steps * heads
    coef = math.log2(math.e) / math.sqrt(queries.shape[2])

    def peer(i):
        return lax.rem(me + 1 + i, n)

    own_q = pltpu.make_async_copy(queries.at[0], qg.at[me], local_sem.at[0])
    get_ku = pltpu.make_async_copy(key_up, ku, local_sem.at[1])
    get_vu = pltpu.make_async_copy(value_up, vu, local_sem.at[2])
    get_op = pltpu.make_async_copy(out_proj, op, local_sem.at[3])
    get_nl = pltpu.make_async_copy(fresh, nl, local_sem.at[4])
    own_q.start()
    get_nl.start()
    get_ku.start()

    def get_cache(b):
        return pltpu.make_async_copy(cache.at[b], kc.at[b], cache_sem.at[b])

    for b in range(reqs):
        get_cache(b).start()
    get_vu.start()
    get_op.start()

    barrier = pltpu.get_barrier_semaphore()

    @pl.loop(0, n - 1)
    def _(i):
        pl.semaphore_signal(barrier, inc=1, device_id={"ctx": peer(i)}, device_id_type=MESH)

    for i in range(1, groups):
        pl.semaphore_signal(
            barrier, inc=1, device_id={"heads": lax.rem(group + i, groups)}, device_id_type=MESH
        )
    pl.semaphore_wait(barrier, n - 1 + groups - 1)

    def send_q(to, slot):
        return pltpu.make_async_remote_copy(
            src_ref=queries.at[0],
            dst_ref=qg.at[slot],
            send_sem=q_send.at[to],
            recv_sem=q_recv.at[slot],
            device_id={"ctx": to},
            device_id_type=MESH,
        )

    @pl.loop(0, n - 1)
    def _(i):
        send_q(peer(i), me).start()

    own_q.wait()

    @pl.loop(0, n - 1)
    def _(i):
        send_q(peer(i), peer(i)).wait_recv()

    @pl.loop(0, rows)
    def _(r):
        block = qg[r]
        at = pl.ds(pl.multiple_of(r * heads, heads), heads)
        qn[at, :] = block[:, :nope].astype(F32)
        qrope[at, : width - latent] = block[:, nope:].astype(F32)
        qfull[at, latent:] = block[:, nope:]

    get_ku.wait()

    @pl.loop(0, heads)
    def _(h):
        x = qn[pl.ds(h, rows, stride=heads), :].astype(BF16)
        y = jnp.dot(x, ku[h], preferred_element_type=F32)
        for c in range(chunks):
            ql[c, pl.ds(h, rows, stride=heads), :] = y[:, c * 128 : (c + 1) * 128]

    @pl.loop(0, reqs)
    def _(b):
        at = pl.ds(pl.multiple_of(b * per, per), per)
        for c in range(chunks):
            qfull[at, c * 128 : (c + 1) * 128] = ql[c, at, :].astype(BF16)

    @pl.loop(0, reqs)
    def _(b):
        get_cache(b).wait()
        at = pl.ds(pl.multiple_of(b * per, per), per)
        s = lax.dot_general(
            qfull[at, :], kc[b], (((1,), (1,)), ((), ())), preferred_element_type=F32
        )
        position = me * keys + lax.broadcasted_iota(jnp.int32, (1, keys), 1)
        s = jnp.where(position < lengths[b], s, NEG)
        m = jnp.max(s, axis=1, keepdims=True)
        p = jnp.exp2((s - m) * coef)
        total = jnp.sum(p, axis=1, keepdims=True)
        o = jnp.dot(p.astype(BF16), kc[b, :, :latent], preferred_element_type=F32)
        for c in range(chunks):
            osum[c, at, :] = o[:, c * 128 : (c + 1) * 128]
        lane = lax.broadcasted_iota(jnp.int32, (per, 128), 1)
        stat[at, :] = jnp.where(lane < rows, m, total)

    get_vu.wait()

    def send_p(to, slot):
        return (
            pltpu.make_async_remote_copy(
                src_ref=sbuf.at[to],
                dst_ref=rbuf.at[slot],
                send_sem=p_send.at[to],
                recv_sem=p_recv.at[slot],
                device_id={"ctx": to},
                device_id_type=MESH,
            ),
            pltpu.make_async_remote_copy(
                src_ref=sstat.at[to],
                dst_ref=rstat.at[slot],
                send_sem=t_send.at[to],
                recv_sem=t_recv.at[slot],
                device_id={"ctx": to},
                device_id_type=MESH,
            ),
        )

    row_of = lax.broadcasted_iota(jnp.int32, (rows, 128), 0)
    lane_of = lax.broadcasted_iota(jnp.int32, (rows, 128), 1)
    diagonal = (lane_of < 2 * rows) & (lax.rem(lane_of, rows) == row_of)

    def partial_of(h):
        x = jnp.concatenate(
            [osum[c, pl.ds(h, rows, stride=heads), :] for c in range(chunks)], axis=1
        ).astype(BF16)
        y = jnp.dot(x, vu[h], preferred_element_type=F32).astype(BF16)
        t = jnp.where(diagonal, stat[pl.ds(h, rows, stride=heads), :], 0.0)
        return y, jnp.sum(t, axis=0, keepdims=True)

    @pl.loop(0, n - 1)
    def _(i):
        h = peer(i)
        y, t = partial_of(h)
        sbuf[h] = y
        sstat[h] = t
        for copy in send_p(h, me):
            copy.start()

    y, t = partial_of(me)
    rbuf[me] = y
    rstat[me] = t

    get_nl.wait()
    mine = jnp.concatenate(
        [ql[c, pl.ds(me, rows, stride=heads), :] for c in range(chunks)], axis=1
    ).astype(BF16)
    mine_rope = qrope[pl.ds(me, rows, stride=heads), :][:, : width - latent].astype(BF16)
    contract = (((1,), (1,)), ((), ()))
    near = lax.dot_general(mine, nl[:, :latent], contract, preferred_element_type=F32)
    near = near + lax.dot_general(mine_rope, nl[:, latent:], contract, preferred_element_type=F32)
    row = lax.broadcasted_iota(jnp.int32, (rows, rows), 0)
    col = lax.broadcasted_iota(jnp.int32, (rows, rows), 1)
    seen = (row // steps == col // steps) & (col <= row)
    near = jnp.where(seen, near, NEG)
    top_near = jnp.max(near, axis=1, keepdims=True)
    w_near = jnp.exp2((near - top_near) * coef)
    total_near = jnp.sum(w_near, axis=1, keepdims=True)
    o_near = jnp.dot(w_near.astype(BF16), nl[:, :latent], preferred_element_type=F32)
    y_near = jnp.dot(o_near.astype(BF16), vu[me], preferred_element_type=F32)

    @pl.loop(0, n - 1)
    def _(i):
        for copy in send_p(peer(i), peer(i)):
            copy.wait_recv()

    turned = jnp.transpose(rstat[:, 0, :])
    tops = turned[:rows, :]
    totals = turned[rows : 2 * rows, :]
    top = jnp.maximum(jnp.max(tops, axis=1, keepdims=True), top_near)
    factor = jnp.exp2((tops - top) * coef)
    factor_near = jnp.exp2((top_near - top) * coef)
    total = jnp.sum(factor * totals, axis=1, keepdims=True) + factor_near * total_near
    acc = y_near * factor_near
    for s in range(n):
        acc = acc + rbuf[s].astype(F32) * factor[:, s : s + 1]
    done = (acc / total).astype(BF16)
    ho[...] = done
    hg[:, pl.ds(pl.multiple_of(me * 128, 128), 128)] = done

    def send_h(to, slot):
        return pltpu.make_async_remote_copy(
            src_ref=ho,
            dst_ref=hg.at[:, pl.ds(pl.multiple_of(slot * 128, 128), 128)],
            send_sem=h_send.at[to],
            recv_sem=h_recv.at[slot],
            device_id={"ctx": to},
            device_id_type=MESH,
        )

    @pl.loop(0, n - 1)
    def _(i):
        send_h(peer(i), me).start()

    get_op.wait()

    @pl.loop(0, n - 1)
    def _(i):
        send_h(peer(i), peer(i)).wait_recv()

    xb[group] = jnp.dot(hg[...], op[...], preferred_element_type=F32)

    def send_x(to, slot):
        return pltpu.make_async_remote_copy(
            src_ref=xb.at[group],
            dst_ref=xb.at[slot],
            send_sem=x_send.at[to],
            recv_sem=x_recv.at[slot],
            device_id={"heads": to},
            device_id_type=MESH,
        )

    for i in range(1, groups):
        send_x(lax.rem(group + i, groups), group).start()
    for i in range(1, groups):
        other = lax.rem(group + i, groups)
        send_x(other, other).wait_recv()
    result = xb[0]
    for g in range(1, groups):
        result = result + xb[g]
    out[...] = result.astype(out.dtype)

    @pl.loop(0, n - 1)
    def _(i):
        to = peer(i)
        send_q(to, me).wait_send()
        for copy in send_p(to, me):
            copy.wait_send()
        send_h(to, me).wait_send()

    for i in range(1, groups):
        send_x(lax.rem(group + i, groups), group).wait_send()


def local(n, groups, queries, cache, fresh, lengths, key_up, value_up, out_proj):
    heads, nope, latent = key_up.shape
    reqs, keys, width = cache.shape
    rows = fresh.shape[0]
    vdim = value_up.shape[2]
    columns = out_proj.shape[1]
    chunks = latent // 128
    hbm = pl.BlockSpec(memory_space=pl.ANY)
    dma = pltpu.SemaphoreType.DMA
    return pl.pallas_call(
        functools.partial(kernel, n, groups, reqs),
        out_shape=jax.ShapeDtypeStruct((rows, columns), BF16),
        in_specs=[hbm, hbm, hbm, pl.BlockSpec(memory_space=pltpu.SMEM), hbm, hbm, hbm],
        out_specs=pl.BlockSpec(memory_space=pltpu.VMEM),
        scratch_shapes=[
            pltpu.VMEM((reqs, keys, width), BF16),
            pltpu.VMEM((heads, nope, latent), BF16),
            pltpu.VMEM((heads, latent, vdim), BF16),
            pltpu.VMEM((heads * vdim, columns), BF16),
            pltpu.VMEM((rows, width), BF16),
            pltpu.VMEM((rows, heads, queries.shape[2]), BF16),
            pltpu.VMEM((rows * heads, nope), F32),
            pltpu.VMEM((rows * heads, 128), F32),
            pltpu.VMEM((chunks, rows * heads, 128), F32),
            pltpu.VMEM((rows * heads, width), BF16),
            pltpu.VMEM((chunks, rows * heads, 128), F32),
            pltpu.VMEM((rows * heads, 128), F32),
            pltpu.VMEM((heads, rows, vdim), BF16),
            pltpu.VMEM((heads, 1, 128), F32),
            pltpu.VMEM((n, rows, vdim), BF16),
            pltpu.VMEM((n, 1, 128), F32),
            pltpu.VMEM((rows, vdim), BF16),
            pltpu.VMEM((rows, heads * vdim), BF16),
            pltpu.VMEM((groups, rows, columns), F32),
            dma((reqs,)),
            dma((5,)),
            dma((n,)),
            dma((n,)),
            dma((n,)),
            dma((n,)),
            dma((n,)),
            dma((n,)),
            dma((n,)),
            dma((n,)),
            dma((groups,)),
            dma((groups,)),
        ],
        compiler_params=pltpu.CompilerParams(
            collective_id=0, has_side_effects=True, vmem_limit_bytes=56 * 1024 * 1024
        ),
        cost_estimate=pl.CostEstimate(
            flops=4 * 10**9, bytes_accessed=25 * 10**6, transcendentals=2 * 10**6
        ),
        name="mla_decode",
    )(queries, cache, fresh, lengths, key_up, value_up, out_proj)


def solution(mesh):
    in_specs = (
        P("ctx", "heads", None),
        P(None, "ctx", None),
        P(),
        P(),
        P("heads", None, None),
        P("heads", None, None),
        P("heads", "ctx"),
    )
    body = functools.partial(local, mesh.shape["ctx"], mesh.shape["heads"])
    return jax.shard_map(
        body, mesh=mesh, in_specs=in_specs, out_specs=P(None, "ctx"), check_vma=False
    )
```

```python
import functools
import math

import jax
import jax.numpy as jnp
from jax import lax
from jax.experimental import pallas as pl
from jax.experimental.pallas import tpu as pltpu
from jax.sharding import PartitionSpec as P

NEG = -3e38
MESH = pl.DeviceIdType.MESH
F32 = jnp.float32
BF16 = jnp.bfloat16


def kernel(
    n,
    groups,
    reqs,
    queries,
    cache,
    fresh,
    lengths,
    key_up,
    value_up,
    out_proj,
    out,
    kc,
    ku,
    vu,
    op,
    nl,
    qg,
    qn,
    qrope,
    ql,
    qfull,
    osum,
    stat,
    sbuf,
    sstat,
    rbuf,
    rstat,
    ho,
    hg,
    xb,
    cache_sem,
    local_sem,
    q_send,
    q_recv,
    p_send,
    p_recv,
    t_send,
    t_recv,
    h_send,
    h_recv,
    x_send,
    x_recv,
):
    me = lax.axis_index("ctx")
    group = lax.axis_index("heads")
    rows = n
    heads = key_up.shape[0]
    nope = key_up.shape[1]
    latent = key_up.shape[2]
    chunks = latent // 128
    width = cache.shape[1]
    keys = cache.shape[2]
    steps = rows // reqs
    per = steps * heads
    contract = (((1,), (1,)), ((), ()))
    coef = math.log2(math.e) / math.sqrt(queries.shape[2])

    def peer(i):
        return lax.rem(me + 1 + i, n)

    own_q = pltpu.make_async_copy(queries.at[0], qg.at[me], local_sem.at[0])
    get_ku = pltpu.make_async_copy(key_up, ku, local_sem.at[1])
    get_vu = pltpu.make_async_copy(value_up, vu, local_sem.at[2])
    get_op = pltpu.make_async_copy(out_proj, op, local_sem.at[3])
    get_nl = pltpu.make_async_copy(fresh, nl, local_sem.at[4])
    own_q.start()
    get_nl.start()
    get_ku.start()

    def get_cache(b):
        return pltpu.make_async_copy(cache.at[b], kc.at[b], cache_sem.at[b])

    for b in range(reqs):
        get_cache(b).start()
    get_vu.start()
    get_op.start()

    barrier = pltpu.get_barrier_semaphore()

    @pl.loop(0, n - 1)
    def _(i):
        pl.semaphore_signal(barrier, inc=1, device_id={"ctx": peer(i)}, device_id_type=MESH)

    for i in range(1, groups):
        pl.semaphore_signal(
            barrier, inc=1, device_id={"heads": lax.rem(group + i, groups)}, device_id_type=MESH
        )
    pl.semaphore_wait(barrier, n - 1 + groups - 1)

    def send_q(to, slot):
        return pltpu.make_async_remote_copy(
            src_ref=queries.at[0],
            dst_ref=qg.at[slot],
            send_sem=q_send.at[to],
            recv_sem=q_recv.at[slot],
            device_id={"ctx": to},
            device_id_type=MESH,
        )

    @pl.loop(0, n - 1)
    def _(i):
        send_q(peer(i), me).start()

    own_q.wait()

    @pl.loop(0, n - 1)
    def _(i):
        send_q(peer(i), peer(i)).wait_recv()

    @pl.loop(0, rows)
    def _(r):
        block = qg[r]
        at = pl.ds(pl.multiple_of(r * heads, heads), heads)
        qn[at, :] = block[:, :nope].astype(F32)
        qrope[at, : width - latent] = block[:, nope:].astype(F32)
        qfull[at, latent:] = block[:, nope:]

    get_ku.wait()

    @pl.loop(0, heads)
    def _(h):
        x = qn[pl.ds(h, rows, stride=heads), :].astype(BF16)
        y = jnp.dot(x, ku[h], preferred_element_type=F32)
        for c in range(chunks):
            ql[c, pl.ds(h, rows, stride=heads), :] = y[:, c * 128 : (c + 1) * 128]

    @pl.loop(0, reqs)
    def _(b):
        at = pl.ds(pl.multiple_of(b * per, per), per)
        for c in range(chunks):
            qfull[at, c * 128 : (c + 1) * 128] = ql[c, at, :].astype(BF16)

    @pl.loop(0, reqs)
    def _(b):
        get_cache(b).wait()
        at = pl.ds(pl.multiple_of(b * per, per), per)
        s = jnp.dot(qfull[at, :], kc[b], preferred_element_type=F32)
        position = me * keys + lax.broadcasted_iota(jnp.int32, (1, keys), 1)
        s = jnp.where(position < lengths[b], s, NEG)
        m = jnp.max(s, axis=1, keepdims=True)
        p = jnp.exp2((s - m) * coef)
        total = jnp.sum(p, axis=1, keepdims=True)
        o = lax.dot_general(
            p.astype(BF16), kc[b, :latent, :], contract, preferred_element_type=F32
        )
        for c in range(chunks):
            osum[c, at, :] = o[:, c * 128 : (c + 1) * 128]
        lane = lax.broadcasted_iota(jnp.int32, (per, 128), 1)
        stat[at, :] = jnp.where(lane < rows, m, total)

    get_vu.wait()

    def send_p(to, slot):
        return (
            pltpu.make_async_remote_copy(
                src_ref=sbuf.at[to],
                dst_ref=rbuf.at[slot],
                send_sem=p_send.at[to],
                recv_sem=p_recv.at[slot],
                device_id={"ctx": to},
                device_id_type=MESH,
            ),
            pltpu.make_async_remote_copy(
                src_ref=sstat.at[to],
                dst_ref=rstat.at[slot],
                send_sem=t_send.at[to],
                recv_sem=t_recv.at[slot],
                device_id={"ctx": to},
                device_id_type=MESH,
            ),
        )

    row_of = lax.broadcasted_iota(jnp.int32, (rows, 128), 0)
    lane_of = lax.broadcasted_iota(jnp.int32, (rows, 128), 1)
    diagonal = (lane_of < 2 * rows) & (lax.rem(lane_of, rows) == row_of)

    def partial_of(h):
        x = jnp.concatenate(
            [osum[c, pl.ds(h, rows, stride=heads), :] for c in range(chunks)], axis=1
        ).astype(BF16)
        y = jnp.dot(x, vu[h], preferred_element_type=F32).astype(BF16)
        t = jnp.where(diagonal, stat[pl.ds(h, rows, stride=heads), :], 0.0)
        return y, jnp.sum(t, axis=0, keepdims=True)

    @pl.loop(0, n - 1)
    def _(i):
        h = peer(i)
        y, t = partial_of(h)
        sbuf[h] = y
        sstat[h] = t
        for copy in send_p(h, me):
            copy.start()

    y, t = partial_of(me)
    rbuf[me] = y
    rstat[me] = t

    get_nl.wait()
    mine = jnp.concatenate(
        [ql[c, pl.ds(me, rows, stride=heads), :] for c in range(chunks)], axis=1
    ).astype(BF16)
    mine_rope = qrope[pl.ds(me, rows, stride=heads), :][:, : width - latent].astype(BF16)
    near = lax.dot_general(mine, nl[:, :latent], contract, preferred_element_type=F32)
    near = near + lax.dot_general(mine_rope, nl[:, latent:], contract, preferred_element_type=F32)
    row = lax.broadcasted_iota(jnp.int32, (rows, rows), 0)
    col = lax.broadcasted_iota(jnp.int32, (rows, rows), 1)
    seen = (row // steps == col // steps) & (col <= row)
    near = jnp.where(seen, near, NEG)
    top_near = jnp.max(near, axis=1, keepdims=True)
    w_near = jnp.exp2((near - top_near) * coef)
    total_near = jnp.sum(w_near, axis=1, keepdims=True)
    o_near = jnp.dot(w_near.astype(BF16), nl[:, :latent], preferred_element_type=F32)
    y_near = jnp.dot(o_near.astype(BF16), vu[me], preferred_element_type=F32)

    @pl.loop(0, n - 1)
    def _(i):
        for copy in send_p(peer(i), peer(i)):
            copy.wait_recv()

    turned = jnp.transpose(rstat[:, 0, :])
    tops = turned[:rows, :]
    totals = turned[rows : 2 * rows, :]
    top = jnp.maximum(jnp.max(tops, axis=1, keepdims=True), top_near)
    factor = jnp.exp2((tops - top) * coef)
    factor_near = jnp.exp2((top_near - top) * coef)
    total = jnp.sum(factor * totals, axis=1, keepdims=True) + factor_near * total_near
    acc = y_near * factor_near
    for s in range(n):
        acc = acc + rbuf[s].astype(F32) * factor[:, s : s + 1]
    done = (acc / total).astype(BF16)
    ho[...] = done
    hg[:, pl.ds(pl.multiple_of(me * 128, 128), 128)] = done

    def send_h(to, slot):
        return pltpu.make_async_remote_copy(
            src_ref=ho,
            dst_ref=hg.at[:, pl.ds(pl.multiple_of(slot * 128, 128), 128)],
            send_sem=h_send.at[to],
            recv_sem=h_recv.at[slot],
            device_id={"ctx": to},
            device_id_type=MESH,
        )

    @pl.loop(0, n - 1)
    def _(i):
        send_h(peer(i), me).start()

    get_op.wait()

    @pl.loop(0, n - 1)
    def _(i):
        send_h(peer(i), peer(i)).wait_recv()

    xb[group] = lax.dot_general(hg[...], op[...], contract, preferred_element_type=F32)

    def send_x(to, slot):
        return pltpu.make_async_remote_copy(
            src_ref=xb.at[group],
            dst_ref=xb.at[slot],
            send_sem=x_send.at[to],
            recv_sem=x_recv.at[slot],
            device_id={"heads": to},
            device_id_type=MESH,
        )

    for i in range(1, groups):
        send_x(lax.rem(group + i, groups), group).start()
    for i in range(1, groups):
        other = lax.rem(group + i, groups)
        send_x(other, other).wait_recv()
    result = xb[0]
    for g in range(1, groups):
        result = result + xb[g]
    out[...] = result.astype(out.dtype)

    @pl.loop(0, n - 1)
    def _(i):
        to = peer(i)
        send_q(to, me).wait_send()
        for copy in send_p(to, me):
            copy.wait_send()
        send_h(to, me).wait_send()

    for i in range(1, groups):
        send_x(lax.rem(group + i, groups), group).wait_send()


def local(n, groups, queries, cache, fresh, lengths, key_up, value_up, out_proj):
    cache = jnp.swapaxes(cache, 1, 2)
    out_proj = jnp.swapaxes(out_proj, 0, 1)
    heads, nope, latent = key_up.shape
    reqs, width, keys = cache.shape
    rows = fresh.shape[0]
    vdim = value_up.shape[2]
    columns = out_proj.shape[0]
    chunks = latent // 128
    hbm = pl.BlockSpec(memory_space=pl.ANY)
    dma = pltpu.SemaphoreType.DMA
    return pl.pallas_call(
        functools.partial(kernel, n, groups, reqs),
        out_shape=jax.ShapeDtypeStruct((rows, columns), BF16),
        in_specs=[hbm, hbm, hbm, pl.BlockSpec(memory_space=pltpu.SMEM), hbm, hbm, hbm],
        out_specs=pl.BlockSpec(memory_space=pltpu.VMEM),
        scratch_shapes=[
            pltpu.VMEM((reqs, width, keys), BF16),
            pltpu.VMEM((heads, nope, latent), BF16),
            pltpu.VMEM((heads, latent, vdim), BF16),
            pltpu.VMEM((columns, heads * vdim), BF16),
            pltpu.VMEM((rows, width), BF16),
            pltpu.VMEM((rows, heads, queries.shape[2]), BF16),
            pltpu.VMEM((rows * heads, nope), F32),
            pltpu.VMEM((rows * heads, 128), F32),
            pltpu.VMEM((chunks, rows * heads, 128), F32),
            pltpu.VMEM((rows * heads, width), BF16),
            pltpu.VMEM((chunks, rows * heads, 128), F32),
            pltpu.VMEM((rows * heads, 128), F32),
            pltpu.VMEM((heads, rows, vdim), BF16),
            pltpu.VMEM((heads, 1, 128), F32),
            pltpu.VMEM((n, rows, vdim), BF16),
            pltpu.VMEM((n, 1, 128), F32),
            pltpu.VMEM((rows, vdim), BF16),
            pltpu.VMEM((rows, heads * vdim), BF16),
            pltpu.VMEM((groups, rows, columns), F32),
            dma((reqs,)),
            dma((5,)),
            dma((n,)),
            dma((n,)),
            dma((n,)),
            dma((n,)),
            dma((n,)),
            dma((n,)),
            dma((n,)),
            dma((n,)),
            dma((groups,)),
            dma((groups,)),
        ],
        compiler_params=pltpu.CompilerParams(
            collective_id=0, has_side_effects=True, vmem_limit_bytes=56 * 1024 * 1024
        ),
        cost_estimate=pl.CostEstimate(
            flops=4 * 10**9, bytes_accessed=25 * 10**6, transcendentals=2 * 10**6
        ),
        name="mla_decode",
    )(queries, cache, fresh, lengths, key_up, value_up, out_proj)


def solution(mesh):
    in_specs = (
        P("ctx", "heads", None),
        P(None, "ctx", None),
        P(),
        P(),
        P("heads", None, None),
        P("heads", None, None),
        P("heads", "ctx"),
    )
    body = functools.partial(local, mesh.shape["ctx"], mesh.shape["heads"])
    return jax.shard_map(
        body, mesh=mesh, in_specs=in_specs, out_specs=P(None, "ctx"), check_vma=False
    )
```

```python
import functools
import math

import jax
import jax.numpy as jnp
from jax import lax
from jax.experimental import pallas as pl
from jax.experimental.pallas import tpu as pltpu
from jax.sharding import PartitionSpec as P

NEG = -3e38
MESH = pl.DeviceIdType.MESH
F32 = jnp.float32
BF16 = jnp.bfloat16
SIDE = 4
LANES = 128


def widen(f):
    halves = []
    for u in range(2):
        halves.append(
            jnp.concatenate(
                [jnp.broadcast_to(f[:, u * 8 + k : u * 8 + k + 1], (8, LANES)) for k in range(8)],
                axis=1,
            )
        )
    return jnp.concatenate(halves, axis=0)


def kernel(
    groups,
    queries,
    cache,
    fresh,
    lengths,
    key_up,
    value_up,
    out_proj,
    out,
    kc,
    ku,
    vu,
    op,
    nl,
    qg,
    qfull,
    perm,
    st,
    stl,
    sr,
    srl,
    cb,
    cbl,
    rb,
    rbl,
    ho,
    hg,
    xb,
    cache_sem,
    local_sem,
    q_send,
    q_recv,
    s_send,
    s_recv,
    r_send,
    r_recv,
    h_send,
    h_recv,
    f_send,
    f_recv,
    x_send,
    x_recv,
):
    me = lax.axis_index("ctx")
    group = lax.axis_index("heads")
    core = lax.rem(me, 2)
    z = lax.rem(me // 2, SIDE)
    y = me // (2 * SIDE)
    rows = fresh.shape[0]
    heads, nope, latent = key_up.shape
    reqs, width, keys = cache.shape
    steps = rows // reqs
    per = steps * heads
    coef = math.log2(math.e) / math.sqrt(queries.shape[2])
    contract = (((1,), (1,)), ((), ()))

    def at(dy, dz, dc=0):
        return (
            lax.rem(y + dy, SIDE) * (2 * SIDE) + lax.rem(z + dz, SIDE) * 2 + lax.rem(core + dc, 2)
        )

    sibling = at(0, 0, 1)
    others = [(dy, dz) for dy in range(SIDE) for dz in range(SIDE) if dy or dz]

    own_q = pltpu.make_async_copy(queries.at[0], qg.at[me], local_sem.at[0])
    get_ku = pltpu.make_async_copy(key_up, ku, local_sem.at[1])
    get_vu = pltpu.make_async_copy(value_up, vu, local_sem.at[2])
    get_op = pltpu.make_async_copy(out_proj, op, local_sem.at[3])
    get_nl = pltpu.make_async_copy(fresh, nl, local_sem.at[4])

    def get_cache(b):
        return pltpu.make_async_copy(cache.at[b], kc.at[b], cache_sem.at[b])

    own_q.start()
    get_nl.start()
    get_ku.start()
    for u in range(2):
        get_cache(2 * y + u).start()
    get_vu.start()

    @pl.loop(2, reqs)
    def _(i):
        get_cache(lax.rem(2 * y + i, reqs)).start()

    get_op.start()

    barrier = pltpu.get_barrier_semaphore()
    rings = [sibling]
    for d in range(1, SIDE):
        rings += [at(0, d), at(d, 0)]
    for to in rings:
        pl.semaphore_signal(barrier, inc=1, device_id={"ctx": to}, device_id_type=MESH)
    for i in range(1, groups):
        pl.semaphore_signal(
            barrier, inc=1, device_id={"heads": lax.rem(group + i, groups)}, device_id_type=MESH
        )
    to_row = lax.broadcasted_iota(jnp.int32, (2 * per, 2 * per), 0)
    of_row = lax.broadcasted_iota(jnp.int32, (2 * per, 2 * per), 1)
    perm[...] = jnp.where(
        of_row == lax.rem(to_row, 2 * steps) * heads + to_row // (2 * steps), 1.0, 0.0
    ).astype(BF16)
    own_q.wait()
    pl.semaphore_wait(barrier, len(rings) + groups - 1)

    def send_q(to, row, k):
        return pltpu.make_async_remote_copy(
            src_ref=qg.at[row],
            dst_ref=qg.at[row],
            send_sem=q_send.at[k],
            recv_sem=q_recv.at[row],
            device_id={"ctx": to},
            device_id_type=MESH,
        )

    q_sends = []
    for d in (1, 3, 2):
        q_sends.append((at(0, d), me))
    for d in (1, 3, 2):
        q_sends.append((at(d, 0), me))
    q_sends.append((sibling, me))
    for dz in (1, 3, 2):
        for d in (1, 3, 2):
            q_sends.append((at(d, 0), at(0, dz)))
        q_sends.append((sibling, at(0, dz)))
    for dy in (1, 3, 2):
        for dz in (0, 1, 3, 2):
            q_sends.append((sibling, at(dy, dz)))
    q_sends = [send_q(to, row, k) for k, (to, row) in enumerate(q_sends)]

    def got_q(row):
        send_q(sibling, row, 0).wait_recv()

    for k in range(7):
        q_sends[k].start()
    for i, dz in enumerate((1, 3, 2)):
        got_q(at(0, dz))
        for k in range(4):
            q_sends[7 + 4 * i + k].start()
    for dz in range(SIDE):
        got_q(at(0, dz, 1))

    sub = lax.broadcasted_iota(jnp.int32, (8, LANES), 0)

    def absorb(pairs):
        starts = [pl.multiple_of(j * 8, 8) for j in pairs]
        many = 8 * len(pairs)
        which = lax.broadcasted_iota(jnp.int32, (many, 8, LANES), 1)
        for two in range(heads // 16):
            span = slice(two * 16, two * 16 + 16)
            x = jnp.concatenate([qg[pl.ds(s, 8), span, :nope] for s in starts], axis=0).astype(F32)
            halves = []
            for u in range(2):
                part = x[:, u * 8 : u * 8 + 8, :]
                wide = jnp.concatenate(
                    [
                        jnp.where(which == k, part, 0.0).reshape(many * 8, LANES).astype(BF16)
                        for k in range(8)
                    ],
                    axis=1,
                )
                first = two * 16 + u * 8
                w = ku[first : first + 8].reshape(8 * nope, latent)
                halves.append(
                    jnp.dot(wide, w, preferred_element_type=F32).reshape(many, 8, latent)
                )
            lat = jnp.concatenate(halves, axis=1).astype(BF16)
            for i, s in enumerate(starts):
                qfull[pl.ds(s, 8), span, :latent] = lat[i * 8 : i * 8 + 8]
        for s in starts:
            qfull[pl.ds(s, 8), :, latent:] = qg[pl.ds(s, 8), :, nope:]

    position = me * keys + lax.broadcasted_iota(jnp.int32, (1, keys), 1)

    def attend(b, near):
        q = qfull[pl.ds(b * steps, steps)].reshape(per, width)
        s = jnp.dot(q, kc[b], preferred_element_type=F32)
        s = jnp.where(position < lengths[b], s, NEG)
        m = jnp.max(s, axis=1, keepdims=True)
        if near:
            n_s = lax.dot_general(q, nl[...], contract, preferred_element_type=F32)
            row = b * steps + lax.broadcasted_iota(jnp.int32, n_s.shape, 0) // heads
            key = lax.broadcasted_iota(jnp.int32, n_s.shape, 1)
            seen = (key >= b * steps) & (key <= row) & (lax.rem(me, 2 * SIDE) == 0)
            n_s = jnp.where(seen, n_s, NEG)
            m = jnp.maximum(m, jnp.max(n_s, axis=1, keepdims=True))
        p = jnp.exp2((s - m) * coef)
        total = jnp.sum(p, axis=1, keepdims=True)
        o = lax.dot_general(
            p.astype(BF16), kc[b, :latent, :], contract, preferred_element_type=F32
        )
        if near:
            n_p = jnp.where(seen, jnp.exp2((n_s - m) * coef), 0.0)
            total = total + jnp.sum(n_p, axis=1, keepdims=True)
            o = o + jnp.dot(n_p.astype(BF16), nl[:, :latent], preferred_element_type=F32)
        return (o / total).astype(BF16), m * coef + jnp.log2(total)

    def to_sibling(p):
        return (
            pltpu.make_async_remote_copy(
                src_ref=st.at[p, 1 - core],
                dst_ref=sr.at[p],
                send_sem=s_send.at[p],
                recv_sem=s_recv.at[p],
                device_id={"ctx": sibling},
                device_id_type=MESH,
            ),
            pltpu.make_async_remote_copy(
                src_ref=stl.at[p, 1 - core],
                dst_ref=srl.at[p],
                send_sem=s_send.at[SIDE + p],
                recv_sem=s_recv.at[SIDE + p],
                device_id={"ctx": sibling},
                device_id_type=MESH,
            ),
        )

    def pair_of(p):
        return lax.rem(y + p, SIDE)

    def work(p, near):
        j = pair_of(p)
        done = []
        for u in range(2):
            get_cache(2 * j + u).wait()
            done.append(attend(2 * j + u, near))
        o = jnp.concatenate([d[0] for d in done], axis=0)
        turned = jnp.dot(perm[...], o, preferred_element_type=F32).astype(BF16)
        log = jnp.concatenate([d[1] for d in done], axis=0)
        h_of = lax.rem(lax.broadcasted_iota(jnp.int32, (2 * per, LANES), 0), heads)
        lane = lax.broadcasted_iota(jnp.int32, (2 * per, LANES), 1)
        log = jnp.sum(jnp.where(h_of == lane, log, 0.0).reshape(8, heads, LANES), axis=1)
        stl[p, 0] = log
        stl[p, 1] = pltpu.roll(log, LANES - 16, 1)
        blocks = []
        for g in range(heads // 8):
            w = jnp.concatenate([vu[g * 8 + k] for k in range(8)], axis=1)
            r = jnp.dot(turned[g * 64 : g * 64 + 64], w, preferred_element_type=F32)
            blocks.append(
                jnp.concatenate(
                    [r[k * 8 : k * 8 + 8, k * LANES : (k + 1) * LANES] for k in range(8)], axis=1
                )
            )
        for c in range(2):
            st[p, c] = jnp.concatenate(blocks[2 * c : 2 * c + 2], axis=0).astype(BF16)
        for copy in to_sibling(p):
            copy.start()

    def to_owner(p, dy):
        j = pair_of(p)
        to_y = lax.rem(y + dy, SIDE)
        to = to_y * (2 * SIDE) + j * 2 + core
        return (
            pltpu.make_async_remote_copy(
                src_ref=cb.at[p, to_y],
                dst_ref=rb.at[me // 2],
                send_sem=r_send.at[p * SIDE + dy],
                recv_sem=r_recv.at[me // 2],
                device_id={"ctx": to},
                device_id_type=MESH,
            ),
            pltpu.make_async_remote_copy(
                src_ref=cbl.at[p],
                dst_ref=rbl.at[me // 2],
                send_sem=r_send.at[16 + p * SIDE + dy],
                recv_sem=r_recv.at[16 + me // 2],
                device_id={"ctx": to},
                device_id_type=MESH,
            ),
        )

    def join(p):
        for copy in to_sibling(p):
            copy.wait_recv()
        la, lb = stl[p, core], srl[p]
        top = jnp.maximum(la, lb)
        wa, wb = jnp.exp2(la - top), jnp.exp2(lb - top)
        both = wa + wb
        cbl[p] = top + jnp.log2(both)
        o = st[p, core].astype(F32) * widen(wa / both) + sr[p].astype(F32) * widen(wb / both)
        o = o.astype(BF16)
        for i in range(SIDE):
            cb[p, i] = o[:, i * 256 : i * 256 + 256]
        mine = pair_of(p) == z

        @pl.when(mine)
        def _():
            rb[me // 2] = cb[p, y]
            rbl[me // 2] = cbl[p]

        @pl.when(jnp.logical_not(mine))
        def _():
            for copy in to_owner(p, 0):
                copy.start()

        for dy in (1, 3, 2):
            for copy in to_owner(p, dy):
                copy.start()

    get_ku.wait()
    absorb([y])
    get_vu.wait()
    get_nl.wait()
    work(0, True)

    k = 19
    for dy in (1, 3, 2):
        for dz in (0, 1, 3, 2):
            got_q(at(dy, dz))
            q_sends[k].start()
            k += 1
    for dy in (1, 3, 2):
        for dz in range(SIDE):
            got_q(at(dy, dz, 1))
    absorb([pair_of(p) for p in range(1, SIDE)])

    @pl.loop(1, SIDE)
    def _(p):
        work(p, False)
        join(p - 1)

    join(SIDE - 1)

    def from_owner(source):
        return (
            pltpu.make_async_remote_copy(
                src_ref=cb.at[0, 0],
                dst_ref=rb.at[source],
                send_sem=r_send.at[0],
                recv_sem=r_recv.at[source],
                device_id={"ctx": sibling},
                device_id_type=MESH,
            ),
            pltpu.make_async_remote_copy(
                src_ref=cbl.at[0],
                dst_ref=rbl.at[source],
                send_sem=r_send.at[0],
                recv_sem=r_recv.at[16 + source],
                device_id={"ctx": sibling},
                device_id_type=MESH,
            ),
        )

    for dy, dz in others:
        for copy in from_owner(at(dy, dz) // 2):
            copy.wait_recv()

    logs = rbl[...]
    top = jnp.max(logs, axis=0)
    w = jnp.exp2(logs - top[None])
    w = w / jnp.sum(w, axis=0)[None]
    acc = jnp.zeros((16, 256), F32)
    for s in range(SIDE * SIDE):
        f = pltpu.roll(w[s], lax.rem(LANES - 2 * y, LANES), 1)
        f = [jnp.broadcast_to(f[:, i : i + 1], (8, LANES)) for i in (0, 1, 8, 9)]
        f = jnp.concatenate(
            [jnp.concatenate(f[:2], axis=1), jnp.concatenate(f[2:], axis=1)], axis=0
        )
        acc = acc + rb[s].astype(F32) * f
    ho[...] = acc.astype(BF16)
    hg[core, z, y] = ho[...]

    def send_h(to, source):
        return pltpu.make_async_remote_copy(
            src_ref=ho,
            dst_ref=hg.at[core, lax.rem(source, SIDE), source // SIDE],
            send_sem=h_send.at[to // 2],
            recv_sem=h_recv.at[source],
            device_id={"ctx": to},
            device_id_type=MESH,
        )

    def forward(of_core, dz):
        slot = lax.rem(z + dz, SIDE)
        return pltpu.make_async_remote_copy(
            src_ref=hg.at[of_core, slot],
            dst_ref=hg.at[of_core, slot],
            send_sem=f_send.at[dz],
            recv_sem=f_recv.at[slot],
            device_id={"ctx": sibling},
            device_id_type=MESH,
        )

    for dy, dz in others:
        send_h(at(dy, dz), me // 2).start()
    for dz in (0, 1, 3, 2):
        for dy in range(SIDE):
            if dy or dz:
                send_h(at(dy, dz), at(dy, dz) // 2).wait_recv()
        forward(core, dz).start()
    get_op.wait()
    for dz in range(SIDE):
        forward(1 - core, dz).wait_recv()

    total = jnp.zeros((rows, out.shape[1]), F32)
    for c in range(2):
        for i in range(SIDE):
            x = [hg[c, pair, i].astype(F32) for pair in range(SIDE)]
            for u in range(2):
                lhs = jnp.concatenate([a[u * 8 : u * 8 + 8] for a in x], axis=0).astype(BF16)
                first = (c * 16 + u * 8 + i * 2) * LANES
                total = total + lax.dot_general(
                    lhs, op[:, first : first + 256], contract, preferred_element_type=F32
                )
    xb[group] = total

    def send_x(to, slot):
        return pltpu.make_async_remote_copy(
            src_ref=xb.at[group],
            dst_ref=xb.at[slot],
            send_sem=x_send.at[to],
            recv_sem=x_recv.at[slot],
            device_id={"heads": to},
            device_id_type=MESH,
        )

    for i in range(1, groups):
        send_x(lax.rem(group + i, groups), group).start()
    for i in range(1, groups):
        other = lax.rem(group + i, groups)
        send_x(other, other).wait_recv()
    result = xb[0]
    for g in range(1, groups):
        result = result + xb[g]
    out[...] = result.astype(out.dtype)

    for copy in q_sends:
        copy.wait_send()
    for p in range(SIDE):
        for copy in to_sibling(p):
            copy.wait_send()

        @pl.when(pair_of(p) != z)
        def _(p=p):
            for copy in to_owner(p, 0):
                copy.wait_send()

        for dy in range(1, SIDE):
            for copy in to_owner(p, dy):
                copy.wait_send()
    for dy, dz in others:
        send_h(at(dy, dz), me // 2).wait_send()
    for dz in range(SIDE):
        forward(core, dz).wait_send()
    for i in range(1, groups):
        send_x(lax.rem(group + i, groups), group).wait_send()


def local(groups, queries, cache, fresh, lengths, key_up, value_up, out_proj):
    cache = jnp.swapaxes(cache, 1, 2)
    out_proj = jnp.swapaxes(out_proj, 0, 1)
    heads, nope, latent = key_up.shape
    reqs, width, keys = cache.shape
    rows = fresh.shape[0]
    vdim = value_up.shape[2]
    columns = out_proj.shape[0]
    per = rows // reqs * heads
    chips = SIDE * SIDE
    hbm = pl.BlockSpec(memory_space=pl.ANY)
    dma = pltpu.SemaphoreType.DMA
    return pl.pallas_call(
        functools.partial(kernel, groups),
        out_shape=jax.ShapeDtypeStruct((rows, columns), BF16),
        in_specs=[hbm, hbm, hbm, pl.BlockSpec(memory_space=pltpu.SMEM), hbm, hbm, hbm],
        out_specs=pl.BlockSpec(memory_space=pltpu.VMEM),
        scratch_shapes=[
            pltpu.VMEM((reqs, width, keys), BF16),
            pltpu.VMEM((heads, nope, latent), BF16),
            pltpu.VMEM((heads, latent, vdim), BF16),
            pltpu.VMEM((columns, heads * vdim), BF16),
            pltpu.VMEM((rows, width), BF16),
            pltpu.VMEM((rows, heads, queries.shape[2]), BF16),
            pltpu.VMEM((rows, heads, width), BF16),
            pltpu.VMEM((2 * per, 2 * per), BF16),
            pltpu.VMEM((SIDE, 2, 16, 1024), BF16),
            pltpu.VMEM((SIDE, 2, 8, LANES), F32),
            pltpu.VMEM((SIDE, 16, 1024), BF16),
            pltpu.VMEM((SIDE, 8, LANES), F32),
            pltpu.VMEM((SIDE, SIDE, 16, 256), BF16),
            pltpu.VMEM((SIDE, 8, LANES), F32),
            pltpu.VMEM((chips, 16, 256), BF16),
            pltpu.VMEM((chips, 8, LANES), F32),
            pltpu.VMEM((16, 256), BF16),
            pltpu.VMEM((2, SIDE, SIDE, 16, 256), BF16),
            pltpu.VMEM((groups, rows, columns), F32),
            dma((reqs,)),
            dma((5,)),
            dma((31,)),
            dma((rows,)),
            dma((2 * SIDE,)),
            dma((2 * SIDE,)),
            dma((2 * chips,)),
            dma((2 * chips,)),
            dma((chips,)),
            dma((chips,)),
            dma((SIDE,)),
            dma((SIDE,)),
            dma((groups,)),
            dma((groups,)),
        ],
        compiler_params=pltpu.CompilerParams(
            collective_id=0, has_side_effects=True, vmem_limit_bytes=56 * 1024 * 1024
        ),
        cost_estimate=pl.CostEstimate(
            flops=4 * 10**9, bytes_accessed=25 * 10**6, transcendentals=2 * 10**6
        ),
        name="mla_decode",
    )(queries, cache, fresh, lengths, key_up, value_up, out_proj)


def solution(mesh):
    in_specs = (
        P("ctx", "heads", None),
        P(None, "ctx", None),
        P(),
        P(),
        P("heads", None, None),
        P("heads", None, None),
        P("heads", "ctx"),
    )
    body = functools.partial(local, mesh.shape["heads"])
    return jax.shard_map(
        body, mesh=mesh, in_specs=in_specs, out_specs=P(None, "ctx"), check_vma=False
    )
```

```python
import functools
import math

import jax
import jax.numpy as jnp
from jax import lax
from jax.experimental import pallas as pl
from jax.experimental.pallas import tpu as pltpu
from jax.sharding import PartitionSpec as P

NEG = -3e38
MESH = pl.DeviceIdType.MESH
F32 = jnp.float32
BF16 = jnp.bfloat16
SIDE = 4
LANES = 128


def widen(f):
    halves = []
    for u in range(2):
        halves.append(
            jnp.concatenate(
                [jnp.broadcast_to(f[:, u * 8 + k : u * 8 + k + 1], (8, LANES)) for k in range(8)],
                axis=1,
            )
        )
    return jnp.concatenate(halves, axis=0)


def kernel(
    groups,
    queries,
    cache,
    fresh,
    lengths_in,
    key_up,
    value_up,
    out_proj,
    out,
    kc,
    ku,
    vu,
    op,
    nl,
    lengths,
    qown,
    qg,
    qfull,
    perm,
    ot,
    tops,
    sums,
    st,
    stl,
    sr,
    srl,
    cb,
    cbl,
    rb,
    rbl,
    ho,
    hg,
    xb,
    cache_sem,
    local_sem,
    q_send,
    q_recv,
    s_send,
    s_recv,
    r_send,
    r_recv,
    h_send,
    h_recv,
    f_send,
    f_recv,
    x_send,
    x_recv,
):
    me = lax.axis_index("ctx")
    group = lax.axis_index("heads")
    core = lax.rem(me, 2)
    z = lax.rem(me // 2, SIDE)
    y = me // (2 * SIDE)
    rows = fresh.shape[0]
    heads, nope, latent = key_up.shape
    reqs, width, keys = cache.shape
    steps = rows // reqs
    per = steps * heads
    coef = math.log2(math.e) / math.sqrt(queries.shape[2])
    contract = (((1,), (1,)), ((), ()))

    def at(dy, dz, dc=0):
        return (
            lax.rem(y + dy, SIDE) * (2 * SIDE) + lax.rem(z + dz, SIDE) * 2 + lax.rem(core + dc, 2)
        )

    sibling = at(0, 0, 1)
    others = [(dy, dz) for dy in range(SIDE) for dz in range(SIDE) if dy or dz]

    own_q = pltpu.make_async_copy(queries.at[0], qown, local_sem.at[0])
    get_ku = pltpu.make_async_copy(key_up, ku, local_sem.at[1])
    get_vu = pltpu.make_async_copy(value_up, vu, local_sem.at[2])
    get_op = pltpu.make_async_copy(out_proj, op, local_sem.at[3])
    get_nl = pltpu.make_async_copy(fresh, nl, local_sem.at[4])
    get_lengths = pltpu.make_async_copy(lengths_in, lengths, local_sem.at[5])

    def get_cache(b):
        return pltpu.make_async_copy(cache.at[b], kc.at[b], cache_sem.at[b])

    own_q.start()
    get_nl.start()
    get_lengths.start()
    get_ku.start()
    for u in range(2):
        get_cache(2 * y + u).start()

    @pl.loop(2, reqs)
    def _(i):
        get_cache(lax.rem(2 * y + i, reqs)).start()

    get_vu.start()
    get_op.start()

    barrier = pltpu.get_barrier_semaphore()
    rings = [sibling]
    for d in range(1, SIDE):
        rings += [at(0, d), at(d, 0)]
    for to in rings:
        pl.semaphore_signal(barrier, inc=1, device_id={"ctx": to}, device_id_type=MESH)
    for i in range(1, groups):
        pl.semaphore_signal(
            barrier, inc=1, device_id={"heads": lax.rem(group + i, groups)}, device_id_type=MESH
        )
    to_row = lax.broadcasted_iota(jnp.int32, (2 * per, 2 * per), 0)
    of_row = lax.broadcasted_iota(jnp.int32, (2 * per, 2 * per), 1)
    perm[...] = jnp.where(
        of_row == (to_row & (2 * steps - 1)) * heads + to_row // (2 * steps), 1.0, 0.0
    ).astype(BF16)
    own_q.wait()
    rope = width - latent
    half = heads // 2
    qg[me, :heads] = qown[:, :nope]
    qg[me, heads:] = jnp.concatenate([qown[:half, nope:], qown[half:, nope:]], axis=1)
    get_lengths.wait()
    pl.semaphore_wait(barrier, len(rings) + groups - 1)

    def send_q(to, row, k):
        return pltpu.make_async_remote_copy(
            src_ref=qg.at[row],
            dst_ref=qg.at[row],
            send_sem=q_send.at[k],
            recv_sem=q_recv.at[row],
            device_id={"ctx": to},
            device_id_type=MESH,
        )

    q_sends = []
    for d in (1, 3, 2):
        q_sends.append((at(0, d), me))
    for d in (1, 3, 2):
        q_sends.append((at(d, 0), me))
    q_sends.append((sibling, me))
    near_rows = [at(d * core, d * (1 - core)) for d in (1, 3, 2)]
    far_rows = [at(d * (1 - core), d * core) for d in (1, 3, 2)]
    for row in near_rows:
        for d in (1, 3, 2):
            q_sends.append((at(d * (1 - core), d * core), row))
        q_sends.append((sibling, row))
    for row in far_rows:
        q_sends.append((sibling, row))
    for dy in (1, 3, 2):
        for dz in (1, 3, 2):
            q_sends.append((sibling, at(dy, dz)))
    q_sends = [send_q(to, row, k) for k, (to, row) in enumerate(q_sends)]

    def got_q(row):
        send_q(sibling, row, 0).wait_recv()

    for k in range(7):
        q_sends[k].start()
    for i, row in enumerate(near_rows):
        got_q(row)
        for k in range(4):
            q_sends[7 + 4 * i + k].start()
    for i, row in enumerate(far_rows):
        got_q(row)
        q_sends[19 + i].start()
    for dz in range(SIDE):
        got_q(at(0, dz, 1))

    def absorb(pairs):
        starts = [pl.multiple_of(j * 8, 8) for j in pairs]
        many = 8 * len(pairs)
        which = lax.broadcasted_iota(jnp.int32, (many, 8, LANES), 1)
        for two in range(heads // 16):
            span = slice(two * 16, two * 16 + 16)
            x = jnp.concatenate([qg[pl.ds(s, 8), span, :] for s in starts], axis=0).astype(F32)
            halves = []
            for u in range(2):
                part = x[:, u * 8 : u * 8 + 8, :]
                wide = jnp.concatenate(
                    [
                        jnp.where(which == k, part, 0.0).reshape(many * 8, LANES).astype(BF16)
                        for k in range(8)
                    ],
                    axis=1,
                )
                first = two * 16 + u * 8
                w = ku[first : first + 8].reshape(8 * nope, latent)
                halves.append(
                    jnp.dot(wide, w, preferred_element_type=F32).reshape(many, 8, latent)
                )
            lat = jnp.concatenate(halves, axis=1).astype(BF16)
            for i, s in enumerate(starts):
                qfull[pl.ds(s, 8), span, :latent] = lat[i * 8 : i * 8 + 8]
        for s in starts:
            qfull[pl.ds(s, 8), :half, latent:] = qg[pl.ds(s, 8), heads:, :rope]
            qfull[pl.ds(s, 8), half:, latent:] = qg[pl.ds(s, 8), heads:, rope:]

    position = me * keys + lax.broadcasted_iota(jnp.int32, (1, keys), 1)

    def attend(b, near):
        q = qfull[pl.ds(b * steps, steps)].reshape(per, width)
        s = jnp.dot(q, kc[b], preferred_element_type=F32)
        s = jnp.where(position < lengths[b], s, NEG)
        m = jnp.max(s, axis=1, keepdims=True)
        if near:
            n_s = lax.dot_general(q, nl[...], contract, preferred_element_type=F32)
            row = b * steps + lax.broadcasted_iota(jnp.int32, n_s.shape, 0) // heads
            key = lax.broadcasted_iota(jnp.int32, n_s.shape, 1)
            seen = (key >= b * steps) & (key <= row) & (lax.rem(me, 2 * SIDE) == 0)
            n_s = jnp.where(seen, n_s, NEG)
            m = jnp.maximum(m, jnp.max(n_s, axis=1, keepdims=True))
        p = jnp.exp2((s - m) * coef)
        total = jnp.sum(p, axis=1, keepdims=True)
        o = lax.dot_general(
            kc[b, :latent, :], p.astype(BF16), contract, preferred_element_type=F32
        )
        if near:
            n_p = jnp.where(seen, jnp.exp2((n_s - m) * coef), 0.0)
            total = total + jnp.sum(n_p, axis=1, keepdims=True)
            o = o + lax.dot_general(
                nl[:, :latent], n_p.astype(BF16), (((0,), (1,)), ((), ())), preferred_element_type=F32
            )
        return o.astype(BF16), m * coef, total

    def to_sibling(p):
        return (
            pltpu.make_async_remote_copy(
                src_ref=st.at[p, 1 - core],
                dst_ref=sr.at[p],
                send_sem=s_send.at[p],
                recv_sem=s_recv.at[p],
                device_id={"ctx": sibling},
                device_id_type=MESH,
            ),
            pltpu.make_async_remote_copy(
                src_ref=stl.at[p, 1 - core],
                dst_ref=srl.at[p],
                send_sem=s_send.at[SIDE + p],
                recv_sem=s_recv.at[SIDE + p],
                device_id={"ctx": sibling},
                device_id_type=MESH,
            ),
        )

    def pair_of(p):
        return lax.rem(y + p, SIDE)

    head_of = lax.broadcasted_iota(jnp.int32, (per, LANES), 0) & (heads - 1)
    lane_of = lax.broadcasted_iota(jnp.int32, (per, LANES), 1)
    lane = lax.broadcasted_iota(jnp.int32, (8, LANES), 1)

    def spread(column):
        one = jnp.where(head_of == lane_of, column, 0.0).reshape(steps, heads, LANES)
        return jnp.sum(one, axis=1)

    def work(p, u, near):
        b = 2 * pair_of(p) + u
        o, m, total = attend(b, near)
        ot[p, :, u * per : (u + 1) * per] = o
        tops[p, u * steps : (u + 1) * steps, :] = spread(m)
        sums[p, u * steps : (u + 1) * steps, :] = spread(total)

    def project(pairs):
        turned = []
        for p in pairs:
            t = lax.dot_general(perm[...], ot[p], contract, preferred_element_type=F32)
            turned.append(t.astype(BF16))
            a, b = tops[p], sums[p]
            stl[p, 0] = jnp.where(lane < 16, a, pltpu.roll(b, 16, 1))
            stl[p, 1] = jnp.where(lane < 16, pltpu.roll(a, LANES - 16, 1), b)
        blocks = [[] for _ in pairs]
        for g in range(heads // 8):
            w = jnp.concatenate([vu[g * 8 + k] for k in range(8)], axis=1)
            x = jnp.concatenate([t[g * 64 : g * 64 + 64] for t in turned], axis=0)
            r = jnp.dot(x, w, preferred_element_type=F32)
            for i in range(len(pairs)):
                part = r[i * 64 : i * 64 + 64]
                blocks[i].append(
                    jnp.concatenate(
                        [part[k * 8 : k * 8 + 8, k * LANES : (k + 1) * LANES] for k in range(8)],
                        axis=1,
                    )
                )
        for i, p in enumerate(pairs):
            for c in range(2):
                st[p, c] = jnp.concatenate(blocks[i][2 * c : 2 * c + 2], axis=0).astype(BF16)
            for copy in to_sibling(p):
                copy.start()

    def to_owner(p, dy):
        j = pair_of(p)
        to_y = lax.rem(y + dy, SIDE)
        to = to_y * (2 * SIDE) + j * 2 + core
        return (
            pltpu.make_async_remote_copy(
                src_ref=cb.at[p, to_y],
                dst_ref=rb.at[me // 2],
                send_sem=r_send.at[p * SIDE + dy],
                recv_sem=r_recv.at[me // 2],
                device_id={"ctx": to},
                device_id_type=MESH,
            ),
            pltpu.make_async_remote_copy(
                src_ref=cbl.at[p],
                dst_ref=rbl.at[me // 2],
                send_sem=r_send.at[16 + p * SIDE + dy],
                recv_sem=r_recv.at[16 + me // 2],
                device_id={"ctx": to},
                device_id_type=MESH,
            ),
        )

    def join(p):
        for copy in to_sibling(p):
            copy.wait_recv()
        la, lb = stl[p, core], srl[p]
        top = jnp.maximum(la, lb)
        wa, wb = jnp.exp2(la - top), jnp.exp2(lb - top)
        both = wa * pltpu.roll(la, LANES - 16, 1) + wb * pltpu.roll(lb, LANES - 16, 1)
        cbl[p] = top + jnp.log2(both)
        o = st[p, core].astype(F32) * widen(wa / both) + sr[p].astype(F32) * widen(wb / both)
        o = o.astype(BF16)
        for i in range(SIDE):
            cb[p, i] = o[:, i * 256 : i * 256 + 256]
        mine = pair_of(p) == z

        @pl.when(mine)
        def _():
            rb[me // 2] = cb[p, y]
            rbl[me // 2] = cbl[p]

        @pl.when(jnp.logical_not(mine))
        def _():
            for copy in to_owner(p, 0):
                copy.start()

        for dy in (1, 3, 2):
            for copy in to_owner(p, dy):
                copy.start()

    get_ku.wait()
    for b in range(reqs):
        get_cache(b).wait()
    get_vu.wait()
    get_op.wait()
    absorb([y])
    get_nl.wait()
    work(0, 0, True)
    work(0, 1, True)

    k = 22
    for dy in (1, 3, 2):
        for dz in (1, 3, 2):
            got_q(at(dy, dz))
            q_sends[k].start()
            k += 1
    for dy in (1, 3, 2):
        for dz in range(SIDE):
            got_q(at(dy, dz, 1))
    absorb([pair_of(p) for p in range(1, SIDE)])

    @pl.loop(1, SIDE - 1)
    def _(p):
        work(p, 0, False)
        work(p, 1, False)

    project(range(SIDE - 1))
    work(SIDE - 1, 0, False)
    for p in range(SIDE - 1):
        join(p)
    work(SIDE - 1, 1, False)
    project([SIDE - 1])
    join(SIDE - 1)

    def from_owner(source):
        return (
            pltpu.make_async_remote_copy(
                src_ref=cb.at[0, 0],
                dst_ref=rb.at[source],
                send_sem=r_send.at[0],
                recv_sem=r_recv.at[source],
                device_id={"ctx": sibling},
                device_id_type=MESH,
            ),
            pltpu.make_async_remote_copy(
                src_ref=cbl.at[0],
                dst_ref=rbl.at[source],
                send_sem=r_send.at[0],
                recv_sem=r_recv.at[16 + source],
                device_id={"ctx": sibling},
                device_id_type=MESH,
            ),
        )

    for dy, dz in others:
        for copy in from_owner(at(dy, dz) // 2):
            copy.wait_recv()

    logs = rbl[...]
    top = jnp.max(logs, axis=0)
    w = jnp.exp2(logs - top[None])
    w = w / jnp.sum(w, axis=0)[None]
    acc = jnp.zeros((16, 256), F32)
    for s in range(SIDE * SIDE):
        f = pltpu.roll(w[s], lax.rem(LANES - 2 * y, LANES), 1)
        f = [jnp.broadcast_to(f[:, i : i + 1], (8, LANES)) for i in (0, 1, 8, 9)]
        f = jnp.concatenate(
            [jnp.concatenate(f[:2], axis=1), jnp.concatenate(f[2:], axis=1)], axis=0
        )
        acc = acc + rb[s].astype(F32) * f
    ho[...] = acc.astype(BF16)
    hg[core, z, y] = ho[...]

    def send_h(to, source):
        return pltpu.make_async_remote_copy(
            src_ref=ho,
            dst_ref=hg.at[core, lax.rem(source, SIDE), source // SIDE],
            send_sem=h_send.at[to // 2],
            recv_sem=h_recv.at[source],
            device_id={"ctx": to},
            device_id_type=MESH,
        )

    def forward(of_core, dz):
        slot = lax.rem(z + dz, SIDE)
        return pltpu.make_async_remote_copy(
            src_ref=hg.at[of_core, slot],
            dst_ref=hg.at[of_core, slot],
            send_sem=f_send.at[dz],
            recv_sem=f_recv.at[slot],
            device_id={"ctx": sibling},
            device_id_type=MESH,
        )

    for dy, dz in others:
        send_h(at(dy, dz), me // 2).start()
    for dz in (0, 1, 3, 2):
        for dy in range(SIDE):
            if dy or dz:
                send_h(at(dy, dz), at(dy, dz) // 2).wait_recv()
        forward(core, dz).start()
    for dz in range(SIDE):
        forward(1 - core, dz).wait_recv()

    total = jnp.zeros((rows, out.shape[1]), F32)
    for c in range(2):
        for i in range(SIDE):
            x = [hg[c, pair, i].astype(F32) for pair in range(SIDE)]
            for u in range(2):
                lhs = jnp.concatenate([a[u * 8 : u * 8 + 8] for a in x], axis=0).astype(BF16)
                first = (c * 16 + u * 8 + i * 2) * LANES
                total = total + lax.dot_general(
                    lhs, op[:, first : first + 256], contract, preferred_element_type=F32
                )
    xb[group] = total.astype(BF16)

    def send_x(to, slot):
        return pltpu.make_async_remote_copy(
            src_ref=xb.at[group],
            dst_ref=xb.at[slot],
            send_sem=x_send.at[to],
            recv_sem=x_recv.at[slot],
            device_id={"heads": to},
            device_id_type=MESH,
        )

    for i in range(1, groups):
        send_x(lax.rem(group + i, groups), group).start()
    for i in range(1, groups):
        other = lax.rem(group + i, groups)
        send_x(other, other).wait_recv()
    result = xb[0].astype(F32)
    for g in range(1, groups):
        result = result + xb[g].astype(F32)
    out[...] = result.astype(out.dtype)

    for copy in q_sends:
        copy.wait_send()
    for p in range(SIDE):
        for copy in to_sibling(p):
            copy.wait_send()

        @pl.when(pair_of(p) != z)
        def _(p=p):
            for copy in to_owner(p, 0):
                copy.wait_send()

        for dy in range(1, SIDE):
            for copy in to_owner(p, dy):
                copy.wait_send()
    for dy, dz in others:
        send_h(at(dy, dz), me // 2).wait_send()
    for dz in range(SIDE):
        forward(core, dz).wait_send()
    for i in range(1, groups):
        send_x(lax.rem(group + i, groups), group).wait_send()


def local(groups, queries, cache, fresh, lengths, key_up, value_up, out_proj):
    cache = jnp.swapaxes(cache, 1, 2)
    out_proj = jnp.swapaxes(out_proj, 0, 1)
    heads, nope, latent = key_up.shape
    reqs, width, keys = cache.shape
    rows = fresh.shape[0]
    vdim = value_up.shape[2]
    columns = out_proj.shape[0]
    per = rows // reqs * heads
    chips = SIDE * SIDE
    hbm = pl.BlockSpec(memory_space=pl.ANY)
    dma = pltpu.SemaphoreType.DMA
    return pl.pallas_call(
        functools.partial(kernel, groups),
        out_shape=jax.ShapeDtypeStruct((rows, columns), BF16),
        in_specs=[hbm] * 7,
        out_specs=pl.BlockSpec(memory_space=pltpu.VMEM),
        scratch_shapes=[
            pltpu.VMEM((reqs, width, keys), BF16),
            pltpu.VMEM((heads, nope, latent), BF16),
            pltpu.VMEM((heads, latent, vdim), BF16),
            pltpu.VMEM((columns, heads * vdim), BF16),
            pltpu.VMEM((rows, width), BF16),
            pltpu.SMEM((reqs,), jnp.int32),
            pltpu.VMEM((heads, queries.shape[2]), BF16),
            pltpu.VMEM((rows, heads + heads // 2, LANES), BF16),
            pltpu.VMEM((rows, heads, width), BF16),
            pltpu.VMEM((2 * per, 2 * per), BF16),
            pltpu.VMEM((SIDE, latent, 2 * per), BF16),
            pltpu.VMEM((SIDE, 8, LANES), F32),
            pltpu.VMEM((SIDE, 8, LANES), F32),
            pltpu.VMEM((SIDE, 2, 16, 1024), BF16),
            pltpu.VMEM((SIDE, 2, 8, LANES), F32),
            pltpu.VMEM((SIDE, 16, 1024), BF16),
            pltpu.VMEM((SIDE, 8, LANES), F32),
            pltpu.VMEM((SIDE, SIDE, 16, 256), BF16),
            pltpu.VMEM((SIDE, 8, LANES), F32),
            pltpu.VMEM((chips, 16, 256), BF16),
            pltpu.VMEM((chips, 8, LANES), F32),
            pltpu.VMEM((16, 256), BF16),
            pltpu.VMEM((2, SIDE, SIDE, 16, 256), BF16),
            pltpu.VMEM((groups, rows, columns), BF16),
            dma((reqs,)),
            dma((6,)),
            dma((31,)),
            dma((rows,)),
            dma((2 * SIDE,)),
            dma((2 * SIDE,)),
            dma((2 * chips,)),
            dma((2 * chips,)),
            dma((chips,)),
            dma((chips,)),
            dma((SIDE,)),
            dma((SIDE,)),
            dma((groups,)),
            dma((groups,)),
        ],
        compiler_params=pltpu.CompilerParams(
            collective_id=0, has_side_effects=True, vmem_limit_bytes=56 * 1024 * 1024
        ),
        cost_estimate=pl.CostEstimate(
            flops=4 * 10**9, bytes_accessed=25 * 10**6, transcendentals=2 * 10**6
        ),
        name="mla_decode",
    )(queries, cache, fresh, lengths, key_up, value_up, out_proj)


def solution(mesh):
    in_specs = (
        P("ctx", "heads", None),
        P(None, "ctx", None),
        P(),
        P(),
        P("heads", None, None),
        P("heads", None, None),
        P("heads", "ctx"),
    )
    body = functools.partial(local, mesh.shape["heads"])
    return jax.shard_map(
        body, mesh=mesh, in_specs=in_specs, out_specs=P(None, "ctx"), check_vma=False
    )
```

```python
import functools
import math

import jax
import jax.numpy as jnp
from jax import lax
from jax.experimental import pallas as pl
from jax.experimental.pallas import tpu as pltpu
from jax.sharding import PartitionSpec as P

NEG = -3e38
MESH = pl.DeviceIdType.MESH
F32 = jnp.float32
BF16 = jnp.bfloat16
SIDE = 4
LANES = 128


def widen(f):
    halves = []
    for u in range(2):
        halves.append(
            jnp.concatenate(
                [jnp.broadcast_to(f[:, u * 8 + k : u * 8 + k + 1], (8, LANES)) for k in range(8)],
                axis=1,
            )
        )
    return jnp.concatenate(halves, axis=0)


def kernel(
    groups,
    queries,
    cache,
    fresh,
    lengths_in,
    key_up,
    value_up,
    out_proj,
    out,
    kc,
    vt,
    ku,
    vu,
    op,
    nl,
    lengths,
    qown,
    qg,
    qfull,
    perm,
    ot,
    tops,
    sums,
    st,
    stl,
    sr,
    srl,
    cb,
    cbl,
    rb,
    rbl,
    ho,
    hg,
    xb,
    cache_sem,
    local_sem,
    q_send,
    q_recv,
    s_send,
    s_recv,
    r_send,
    r_recv,
    h_send,
    h_recv,
    f_send,
    f_recv,
    x_send,
    x_recv,
):
    me = lax.axis_index("ctx")
    group = lax.axis_index("heads")
    core = lax.rem(me, 2)
    z = lax.rem(me // 2, SIDE)
    y = me // (2 * SIDE)
    rows = fresh.shape[0]
    heads, nope, latent = key_up.shape
    reqs, width, keys = cache.shape
    steps = rows // reqs
    per = steps * heads
    coef = math.log2(math.e) / math.sqrt(queries.shape[2])
    contract = (((1,), (1,)), ((), ()))

    def at(dy, dz, dc=0):
        return (
            lax.rem(y + dy, SIDE) * (2 * SIDE) + lax.rem(z + dz, SIDE) * 2 + lax.rem(core + dc, 2)
        )

    sibling = at(0, 0, 1)
    others = [(dy, dz) for dy in range(SIDE) for dz in range(SIDE) if dy or dz]

    own_q = pltpu.make_async_copy(queries.at[0], qown, local_sem.at[0])
    get_ku = pltpu.make_async_copy(key_up, ku, local_sem.at[1])
    get_vu = pltpu.make_async_copy(value_up, vu, local_sem.at[2])
    get_op = pltpu.make_async_copy(out_proj, op, local_sem.at[3])
    get_nl = pltpu.make_async_copy(fresh, nl, local_sem.at[4])
    get_lengths = pltpu.make_async_copy(lengths_in, lengths, local_sem.at[5])

    def get_cache(b):
        return pltpu.make_async_copy(cache.at[b], kc.at[b], cache_sem.at[b])

    own_q.start()
    get_nl.start()
    get_lengths.start()
    get_ku.start()
    for u in range(2):
        get_cache(2 * y + u).start()

    @pl.loop(2, reqs)
    def _(i):
        get_cache(lax.rem(2 * y + i, reqs)).start()

    get_vu.start()
    get_op.start()

    barrier = pltpu.get_barrier_semaphore()
    peers = [sibling] + [at(dy, dz) for dy, dz in others]
    for to in peers:
        pl.semaphore_signal(barrier, inc=1, device_id={"ctx": to}, device_id_type=MESH)
    for i in range(1, groups):
        pl.semaphore_signal(
            barrier, inc=1, device_id={"heads": lax.rem(group + i, groups)}, device_id_type=MESH
        )
    to_row = lax.broadcasted_iota(jnp.int32, (2 * per, 2 * per), 0)
    of_row = lax.broadcasted_iota(jnp.int32, (2 * per, 2 * per), 1)
    perm[...] = jnp.where(
        of_row == (to_row & (2 * steps - 1)) * heads + to_row // (2 * steps), 1.0, 0.0
    ).astype(BF16)
    own_q.wait()
    rope = width - latent
    half = heads // 2
    qg[me, :heads] = qown[:, :nope]
    qg[me, heads:] = jnp.concatenate([qown[:half, nope:], qown[half:, nope:]], axis=1)
    get_lengths.wait()
    pl.semaphore_wait(barrier, len(peers) + groups - 1)

    def send_q(to, row, k):
        return pltpu.make_async_remote_copy(
            src_ref=qg.at[row],
            dst_ref=qg.at[row],
            send_sem=q_send.at[k],
            recv_sem=q_recv.at[row],
            device_id={"ctx": to},
            device_id_type=MESH,
        )

    along_z = [(0, 1), (0, 3), (0, 2)]
    across = [(2, 2), (2, 1), (2, 3), (1, 2), (3, 2), (1, 1), (1, 3), (3, 1), (3, 3)]
    across += [(2, 0), (1, 0), (3, 0)]
    q_sends = [(sibling, me)] + [(at(dy, dz), me) for dy, dz in along_z + across]
    q_sends += [(sibling, at(dy, dz)) for dy, dz in along_z + across[::-1]]
    q_sends = [send_q(to, row, k) for k, (to, row) in enumerate(q_sends)]

    def got_q(row):
        send_q(sibling, row, 0).wait_recv()

    for k in range(16):
        q_sends[k].start()

    @pl.loop(0, reqs)
    def _(i):
        b = lax.rem(2 * y + i, reqs)
        get_cache(b).wait()
        for c in range(latent // LANES):
            vt[b, :, c * LANES : (c + 1) * LANES] = jnp.transpose(
                kc[b, c * LANES : (c + 1) * LANES, :]
            )

    for i, (dy, dz) in enumerate(along_z):
        got_q(at(dy, dz))
        q_sends[16 + i].start()
    for dz in range(SIDE):
        got_q(at(0, dz, 1))

    def absorb(pairs):
        starts = [pl.multiple_of(j * 8, 8) for j in pairs]
        many = 8 * len(pairs)
        which = lax.broadcasted_iota(jnp.int32, (many, 8, LANES), 1)
        for two in range(heads // 16):
            span = slice(two * 16, two * 16 + 16)
            x = jnp.concatenate([qg[pl.ds(s, 8), span, :] for s in starts], axis=0).astype(F32)
            halves = []
            for u in range(2):
                part = x[:, u * 8 : u * 8 + 8, :]
                wide = jnp.concatenate(
                    [
                        jnp.where(which == k, part, 0.0).reshape(many * 8, LANES).astype(BF16)
                        for k in range(8)
                    ],
                    axis=1,
                )
                first = two * 16 + u * 8
                w = ku[first : first + 8].reshape(8 * nope, latent)
                halves.append(
                    jnp.dot(wide, w, preferred_element_type=F32).reshape(many, 8, latent)
                )
            lat = jnp.concatenate(halves, axis=1).astype(BF16)
            for i, s in enumerate(starts):
                qfull[pl.ds(s, 8), span, :latent] = lat[i * 8 : i * 8 + 8]
        for s in starts:
            qfull[pl.ds(s, 8), :half, latent:] = qg[pl.ds(s, 8), heads:, :rope]
            qfull[pl.ds(s, 8), half:, latent:] = qg[pl.ds(s, 8), heads:, rope:]

    position = me * keys + lax.broadcasted_iota(jnp.int32, (1, keys), 1)

    def attend(b, near):
        q = qfull[pl.ds(b * steps, steps)].reshape(per, width)
        s = jnp.dot(q, kc[b], preferred_element_type=F32)
        s = jnp.where(position < lengths[b], s, NEG)
        m = jnp.max(s, axis=1, keepdims=True)
        if near:
            n_s = lax.dot_general(q, nl[...], contract, preferred_element_type=F32)
            row = b * steps + lax.broadcasted_iota(jnp.int32, n_s.shape, 0) // heads
            key = lax.broadcasted_iota(jnp.int32, n_s.shape, 1)
            seen = (key >= b * steps) & (key <= row) & (lax.rem(me, 2 * SIDE) == 0)
            n_s = jnp.where(seen, n_s, NEG)
            m = jnp.maximum(m, jnp.max(n_s, axis=1, keepdims=True))
        p = jnp.exp2((s - m) * coef)
        total = jnp.sum(p, axis=1, keepdims=True)
        o = jnp.dot(p.astype(BF16), vt[b], preferred_element_type=F32)
        if near:
            n_p = jnp.where(seen, jnp.exp2((n_s - m) * coef), 0.0)
            total = total + jnp.sum(n_p, axis=1, keepdims=True)
            o = o + jnp.dot(n_p.astype(BF16), nl[:, :latent], preferred_element_type=F32)
        return o.astype(BF16), m * coef, total

    def to_sibling(p):
        return (
            pltpu.make_async_remote_copy(
                src_ref=st.at[p, 1 - core],
                dst_ref=sr.at[p],
                send_sem=s_send.at[p],
                recv_sem=s_recv.at[p],
                device_id={"ctx": sibling},
                device_id_type=MESH,
            ),
            pltpu.make_async_remote_copy(
                src_ref=stl.at[p, 1 - core],
                dst_ref=srl.at[p],
                send_sem=s_send.at[SIDE + p],
                recv_sem=s_recv.at[SIDE + p],
                device_id={"ctx": sibling},
                device_id_type=MESH,
            ),
        )

    def pair_of(p):
        return lax.rem(y + p, SIDE)

    head_of = lax.broadcasted_iota(jnp.int32, (per, LANES), 0) & (heads - 1)
    lane_of = lax.broadcasted_iota(jnp.int32, (per, LANES), 1)
    lane = lax.broadcasted_iota(jnp.int32, (8, LANES), 1)

    def spread(column):
        one = jnp.where(head_of == lane_of, column, 0.0).reshape(steps, heads, LANES)
        return jnp.sum(one, axis=1)

    def work(p, u, near):
        b = 2 * pair_of(p) + u
        o, m, total = attend(b, near)
        ot[p, u * per : (u + 1) * per, :] = o
        tops[p, u * steps : (u + 1) * steps, :] = spread(m)
        sums[p, u * steps : (u + 1) * steps, :] = spread(total)

    def project(pairs):
        turned = []
        for p in pairs:
            t = jnp.dot(perm[...], ot[p], preferred_element_type=F32)
            turned.append(t.astype(BF16))
            a, b = tops[p], sums[p]
            stl[p, 0] = jnp.where(lane < 16, a, pltpu.roll(b, 16, 1))
            stl[p, 1] = jnp.where(lane < 16, pltpu.roll(a, LANES - 16, 1), b)
        blocks = [[] for _ in pairs]
        for g in range(heads // 8):
            w = jnp.concatenate([vu[g * 8 + k] for k in range(8)], axis=1)
            x = jnp.concatenate([t[g * 64 : g * 64 + 64] for t in turned], axis=0)
            r = jnp.dot(x, w, preferred_element_type=F32)
            for i in range(len(pairs)):
                part = r[i * 64 : i * 64 + 64]
                blocks[i].append(
                    jnp.concatenate(
                        [part[k * 8 : k * 8 + 8, k * LANES : (k + 1) * LANES] for k in range(8)],
                        axis=1,
                    )
                )
        for i, p in enumerate(pairs):
            for c in range(2):
                st[p, c] = jnp.concatenate(blocks[i][2 * c : 2 * c + 2], axis=0).astype(BF16)
            for copy in to_sibling(p):
                copy.start()

    def to_owner(p, dy):
        j = pair_of(p)
        to_y = lax.rem(y + dy, SIDE)
        to = to_y * (2 * SIDE) + j * 2 + core
        return (
            pltpu.make_async_remote_copy(
                src_ref=cb.at[p, to_y],
                dst_ref=rb.at[me // 2],
                send_sem=r_send.at[p * SIDE + dy],
                recv_sem=r_recv.at[me // 2],
                device_id={"ctx": to},
                device_id_type=MESH,
            ),
            pltpu.make_async_remote_copy(
                src_ref=cbl.at[p],
                dst_ref=rbl.at[me // 2],
                send_sem=r_send.at[16 + p * SIDE + dy],
                recv_sem=r_recv.at[16 + me // 2],
                device_id={"ctx": to},
                device_id_type=MESH,
            ),
        )

    def join(p):
        for copy in to_sibling(p):
            copy.wait_recv()
        la, lb = stl[p, core], srl[p]
        top = jnp.maximum(la, lb)
        wa, wb = jnp.exp2(la - top), jnp.exp2(lb - top)
        both = wa * pltpu.roll(la, LANES - 16, 1) + wb * pltpu.roll(lb, LANES - 16, 1)
        cbl[p] = top + jnp.log2(both)
        o = st[p, core].astype(F32) * widen(wa / both) + sr[p].astype(F32) * widen(wb / both)
        o = o.astype(BF16)
        for i in range(SIDE):
            cb[p, i] = o[:, i * 256 : i * 256 + 256]
        mine = pair_of(p) == z

        @pl.when(mine)
        def _():
            rb[me // 2] = cb[p, y]
            rbl[me // 2] = cbl[p]

        @pl.when(jnp.logical_not(mine))
        def _():
            for copy in to_owner(p, 0):
                copy.start()

        for dy in (1, 3, 2):
            for copy in to_owner(p, dy):
                copy.start()

    get_ku.wait()
    get_nl.wait()
    get_vu.wait()
    get_op.wait()
    absorb([y])
    for i, (dy, dz) in enumerate(across[::-1]):
        got_q(at(dy, dz))
        q_sends[19 + i].start()
    work(0, 0, True)
    for dy in range(1, SIDE):
        for dz in range(SIDE):
            got_q(at(dy, dz, 1))
    absorb([pair_of(p) for p in range(1, SIDE)])
    work(0, 1, True)
    @pl.loop(1, SIDE - 1)
    def _(p):
        work(p, 0, False)
        work(p, 1, False)

    project(range(SIDE - 1))
    work(SIDE - 1, 0, False)
    for p in range(SIDE - 1):
        join(p)
    work(SIDE - 1, 1, False)
    project([SIDE - 1])
    join(SIDE - 1)

    def from_owner(source):
        return (
            pltpu.make_async_remote_copy(
                src_ref=cb.at[0, 0],
                dst_ref=rb.at[source],
                send_sem=r_send.at[0],
                recv_sem=r_recv.at[source],
                device_id={"ctx": sibling},
                device_id_type=MESH,
            ),
            pltpu.make_async_remote_copy(
                src_ref=cbl.at[0],
                dst_ref=rbl.at[source],
                send_sem=r_send.at[0],
                recv_sem=r_recv.at[16 + source],
                device_id={"ctx": sibling},
                device_id_type=MESH,
            ),
        )

    for dy, dz in others:
        for copy in from_owner(at(dy, dz) // 2):
            copy.wait_recv()

    logs = rbl[...]
    top = jnp.max(logs, axis=0)
    w = jnp.exp2(logs - top[None])
    w = w / jnp.sum(w, axis=0)[None]
    acc = jnp.zeros((16, 256), F32)
    for s in range(SIDE * SIDE):
        f = pltpu.roll(w[s], lax.rem(LANES - 2 * y, LANES), 1)
        f = [jnp.broadcast_to(f[:, i : i + 1], (8, LANES)) for i in (0, 1, 8, 9)]
        f = jnp.concatenate(
            [jnp.concatenate(f[:2], axis=1), jnp.concatenate(f[2:], axis=1)], axis=0
        )
        acc = acc + rb[s].astype(F32) * f
    ho[...] = acc.astype(BF16)
    hg[core, z, y] = ho[...]

    def send_h(to, source):
        return pltpu.make_async_remote_copy(
            src_ref=ho,
            dst_ref=hg.at[core, lax.rem(source, SIDE), source // SIDE],
            send_sem=h_send.at[to // 2],
            recv_sem=h_recv.at[source],
            device_id={"ctx": to},
            device_id_type=MESH,
        )

    def forward(of_core, dz):
        slot = lax.rem(z + dz, SIDE)
        return pltpu.make_async_remote_copy(
            src_ref=hg.at[of_core, slot],
            dst_ref=hg.at[of_core, slot],
            send_sem=f_send.at[dz],
            recv_sem=f_recv.at[slot],
            device_id={"ctx": sibling},
            device_id_type=MESH,
        )

    for dy, dz in others:
        send_h(at(dy, dz), me // 2).start()
    for dz in (0, 1, 3, 2):
        for dy in range(SIDE):
            if dy or dz:
                send_h(at(dy, dz), at(dy, dz) // 2).wait_recv()
        forward(core, dz).start()
    for dz in range(SIDE):
        forward(1 - core, dz).wait_recv()

    total = jnp.zeros((rows, out.shape[1]), F32)
    for c in range(2):
        for i in range(SIDE):
            x = [hg[c, pair, i].astype(F32) for pair in range(SIDE)]
            for u in range(2):
                lhs = jnp.concatenate([a[u * 8 : u * 8 + 8] for a in x], axis=0).astype(BF16)
                first = (c * 16 + u * 8 + i * 2) * LANES
                total = total + lax.dot_general(
                    lhs, op[:, first : first + 256], contract, preferred_element_type=F32
                )
    xb[group] = total.astype(BF16)

    def send_x(to, slot):
        return pltpu.make_async_remote_copy(
            src_ref=xb.at[group],
            dst_ref=xb.at[slot],
            send_sem=x_send.at[to],
            recv_sem=x_recv.at[slot],
            device_id={"heads": to},
            device_id_type=MESH,
        )

    for i in range(1, groups):
        send_x(lax.rem(group + i, groups), group).start()
    for i in range(1, groups):
        other = lax.rem(group + i, groups)
        send_x(other, other).wait_recv()
    result = xb[0].astype(F32)
    for g in range(1, groups):
        result = result + xb[g].astype(F32)
    out[...] = result.astype(out.dtype)

    for copy in q_sends:
        copy.wait_send()
    for p in range(SIDE):
        for copy in to_sibling(p):
            copy.wait_send()

        @pl.when(pair_of(p) != z)
        def _(p=p):
            for copy in to_owner(p, 0):
                copy.wait_send()

        for dy in range(1, SIDE):
            for copy in to_owner(p, dy):
                copy.wait_send()
    for dy, dz in others:
        send_h(at(dy, dz), me // 2).wait_send()
    for dz in range(SIDE):
        forward(core, dz).wait_send()
    for i in range(1, groups):
        send_x(lax.rem(group + i, groups), group).wait_send()


def local(groups, queries, cache, fresh, lengths, key_up, value_up, out_proj):
    cache = jnp.swapaxes(cache, 1, 2)
    out_proj = jnp.swapaxes(out_proj, 0, 1)
    heads, nope, latent = key_up.shape
    reqs, width, keys = cache.shape
    rows = fresh.shape[0]
    vdim = value_up.shape[2]
    columns = out_proj.shape[0]
    per = rows // reqs * heads
    chips = SIDE * SIDE
    hbm = pl.BlockSpec(memory_space=pl.ANY)
    dma = pltpu.SemaphoreType.DMA
    return pl.pallas_call(
        functools.partial(kernel, groups),
        out_shape=jax.ShapeDtypeStruct((rows, columns), BF16),
        in_specs=[hbm] * 7,
        out_specs=pl.BlockSpec(memory_space=pltpu.VMEM),
        scratch_shapes=[
            pltpu.VMEM((reqs, width, keys), BF16),
            pltpu.VMEM((reqs, keys, latent), BF16),
            pltpu.VMEM((heads, nope, latent), BF16),
            pltpu.VMEM((heads, latent, vdim), BF16),
            pltpu.VMEM((columns, heads * vdim), BF16),
            pltpu.VMEM((rows, width), BF16),
            pltpu.SMEM((reqs,), jnp.int32),
            pltpu.VMEM((heads, queries.shape[2]), BF16),
            pltpu.VMEM((rows, heads + heads // 2, LANES), BF16),
            pltpu.VMEM((rows, heads, width), BF16),
            pltpu.VMEM((2 * per, 2 * per), BF16),
            pltpu.VMEM((SIDE, 2 * per, latent), BF16),
            pltpu.VMEM((SIDE, 8, LANES), F32),
            pltpu.VMEM((SIDE, 8, LANES), F32),
            pltpu.VMEM((SIDE, 2, 16, 1024), BF16),
            pltpu.VMEM((SIDE, 2, 8, LANES), F32),
            pltpu.VMEM((SIDE, 16, 1024), BF16),
            pltpu.VMEM((SIDE, 8, LANES), F32),
            pltpu.VMEM((SIDE, SIDE, 16, 256), BF16),
            pltpu.VMEM((SIDE, 8, LANES), F32),
            pltpu.VMEM((chips, 16, 256), BF16),
            pltpu.VMEM((chips, 8, LANES), F32),
            pltpu.VMEM((16, 256), BF16),
            pltpu.VMEM((2, SIDE, SIDE, 16, 256), BF16),
            pltpu.VMEM((groups, rows, columns), BF16),
            dma((reqs,)),
            dma((6,)),
            dma((31,)),
            dma((rows,)),
            dma((2 * SIDE,)),
            dma((2 * SIDE,)),
            dma((2 * chips,)),
            dma((2 * chips,)),
            dma((chips,)),
            dma((chips,)),
            dma((SIDE,)),
            dma((SIDE,)),
            dma((groups,)),
            dma((groups,)),
        ],
        compiler_params=pltpu.CompilerParams(
            collective_id=0, has_side_effects=True, vmem_limit_bytes=56 * 1024 * 1024
        ),
        cost_estimate=pl.CostEstimate(
            flops=4 * 10**9, bytes_accessed=25 * 10**6, transcendentals=2 * 10**6
        ),
        name="mla_decode",
    )(queries, cache, fresh, lengths, key_up, value_up, out_proj)


def solution(mesh):
    in_specs = (
        P("ctx", "heads", None),
        P(None, "ctx", None),
        P(),
        P(),
        P("heads", None, None),
        P("heads", None, None),
        P("heads", "ctx"),
    )
    body = functools.partial(local, mesh.shape["heads"])
    return jax.shard_map(
        body, mesh=mesh, in_specs=in_specs, out_specs=P(None, "ctx"), check_vma=False
    )
```

```python
import functools
import math

import jax
import jax.numpy as jnp
from jax import lax
from jax.experimental import pallas as pl
from jax.experimental.pallas import tpu as pltpu
from jax.sharding import PartitionSpec as P

NEG = -3e38
MESH = pl.DeviceIdType.MESH
F32 = jnp.float32
BF16 = jnp.bfloat16
SIDE = 4
LANES = 128


def kernel(
    groups,
    queries,
    cache,
    fresh,
    lengths_in,
    key_up,
    value_up,
    out_proj,
    out,
    kc,
    vt,
    ku,
    vu,
    op,
    nl,
    lengths,
    qown,
    qg,
    qfull,
    perm,
    ot,
    tops,
    sums,
    st,
    stl,
    rb,
    rbl,
    ho,
    hg,
    xb,
    cache_sem,
    local_sem,
    q_send,
    q_recv,
    r_send,
    r_recv,
    h_send,
    h_recv,
    x_send,
    x_recv,
):
    me = lax.axis_index("ctx")
    group = lax.axis_index("heads")
    core = lax.rem(me, 2)
    z = lax.rem(me // 2, SIDE)
    y = me // (2 * SIDE)
    rows = fresh.shape[0]
    heads, nope, latent = key_up.shape
    reqs, width, keys = cache.shape
    steps = rows // reqs
    per = steps * heads
    coef = math.log2(math.e) / math.sqrt(queries.shape[2])
    contract = (((1,), (1,)), ((), ()))

    def at(dy, dz, dc=0):
        return (
            lax.rem(y + dy, SIDE) * (2 * SIDE) + lax.rem(z + dz, SIDE) * 2 + lax.rem(core + dc, 2)
        )

    sibling = at(0, 0, 1)
    others = [(dy, dz) for dy in range(SIDE) for dz in range(SIDE) if dy or dz]
    hops = (0, 1, 2, 1)
    everyone = [(dy, dz, dc) for dy, dz in [(0, 0)] + others for dc in range(2) if dy or dz or dc]
    everyone.sort(key=lambda d: -hops[d[0]] - hops[d[1]])

    own_q = pltpu.make_async_copy(queries.at[0], qown, local_sem.at[0])
    get_ku = pltpu.make_async_copy(key_up, ku, local_sem.at[1])
    get_vu = pltpu.make_async_copy(value_up, vu, local_sem.at[2])
    get_op = pltpu.make_async_copy(out_proj, op, local_sem.at[3])
    get_nl = pltpu.make_async_copy(fresh, nl, local_sem.at[4])
    get_lengths = pltpu.make_async_copy(lengths_in, lengths, local_sem.at[5])

    def get_cache(b):
        return pltpu.make_async_copy(cache.at[b], kc.at[b], cache_sem.at[b])

    own_q.start()
    get_nl.start()
    get_lengths.start()
    get_ku.start()
    for u in range(2):
        get_cache(2 * y + u).start()

    @pl.loop(2, reqs)
    def _(i):
        get_cache(lax.rem(2 * y + i, reqs)).start()

    get_vu.start()
    get_op.start()

    barrier = pltpu.get_barrier_semaphore()
    peers = [sibling] + [at(dy, dz) for dy, dz in others]
    for to in peers:
        pl.semaphore_signal(barrier, inc=1, device_id={"ctx": to}, device_id_type=MESH)
    for i in range(1, groups):
        pl.semaphore_signal(
            barrier, inc=1, device_id={"heads": lax.rem(group + i, groups)}, device_id_type=MESH
        )
    to_row = lax.broadcasted_iota(jnp.int32, (2 * per, 2 * per), 0)
    of_row = lax.broadcasted_iota(jnp.int32, (2 * per, 2 * per), 1)
    perm[...] = jnp.where(
        of_row == (to_row & (2 * steps - 1)) * heads + to_row // (2 * steps), 1.0, 0.0
    ).astype(BF16)
    own_q.wait()
    rope = width - latent
    half = heads // 2
    qg[me, :heads] = qown[:, :nope]
    qg[me, heads:] = jnp.concatenate([qown[:half, nope:], qown[half:, nope:]], axis=1)
    get_lengths.wait()
    pl.semaphore_wait(barrier, len(peers) + groups - 1)

    def send_q(to, row, k):
        return pltpu.make_async_remote_copy(
            src_ref=qg.at[row],
            dst_ref=qg.at[row],
            send_sem=q_send.at[k],
            recv_sem=q_recv.at[row],
            device_id={"ctx": to},
            device_id_type=MESH,
        )

    along_z = [(0, 1), (0, 3), (0, 2)]
    across = [(2, 2), (2, 1), (2, 3), (1, 2), (3, 2), (1, 1), (1, 3), (3, 1), (3, 3)]
    across += [(2, 0), (1, 0), (3, 0)]
    q_sends = [(sibling, me)] + [(at(dy, dz), me) for dy, dz in along_z + across]
    q_sends += [(sibling, at(dy, dz)) for dy, dz in along_z + across[::-1]]
    q_sends = [send_q(to, row, k) for k, (to, row) in enumerate(q_sends)]

    def got_q(row):
        send_q(sibling, row, 0).wait_recv()

    for k in range(16):
        q_sends[k].start()

    @pl.loop(0, reqs)
    def _(i):
        b = lax.rem(2 * y + i, reqs)
        get_cache(b).wait()
        for c in range(latent // LANES):
            vt[b, :, c * LANES : (c + 1) * LANES] = jnp.transpose(
                kc[b, c * LANES : (c + 1) * LANES, :]
            )

    for i, (dy, dz) in enumerate(along_z):
        got_q(at(dy, dz))
        q_sends[16 + i].start()
    for dz in range(SIDE):
        got_q(at(0, dz, 1))

    def absorb(pairs):
        starts = [pl.multiple_of(j * 8, 8) for j in pairs]
        many = 8 * len(pairs)
        which = lax.broadcasted_iota(jnp.int32, (many, 8, LANES), 1)
        for two in range(heads // 16):
            span = slice(two * 16, two * 16 + 16)
            x = jnp.concatenate([qg[pl.ds(s, 8), span, :] for s in starts], axis=0).astype(F32)
            halves = []
            for u in range(2):
                part = x[:, u * 8 : u * 8 + 8, :]
                wide = jnp.concatenate(
                    [
                        jnp.where(which == k, part, 0.0).reshape(many * 8, LANES).astype(BF16)
                        for k in range(8)
                    ],
                    axis=1,
                )
                first = two * 16 + u * 8
                w = ku[first : first + 8].reshape(8 * nope, latent)
                halves.append(
                    jnp.dot(wide, w, preferred_element_type=F32).reshape(many, 8, latent)
                )
            lat = jnp.concatenate(halves, axis=1).astype(BF16)
            for i, s in enumerate(starts):
                qfull[pl.ds(s, 8), span, :latent] = lat[i * 8 : i * 8 + 8]
        for s in starts:
            qfull[pl.ds(s, 8), :half, latent:] = qg[pl.ds(s, 8), heads:, :rope]
            qfull[pl.ds(s, 8), half:, latent:] = qg[pl.ds(s, 8), heads:, rope:]

    position = me * keys + lax.broadcasted_iota(jnp.int32, (1, keys), 1)

    def attend(b, near):
        q = qfull[pl.ds(b * steps, steps)].reshape(per, width)
        s = jnp.dot(q, kc[b], preferred_element_type=F32)
        s = jnp.where(position < lengths[b], s, NEG)
        m = jnp.max(s, axis=1, keepdims=True)
        if near:
            n_s = lax.dot_general(q, nl[...], contract, preferred_element_type=F32)
            row = b * steps + lax.broadcasted_iota(jnp.int32, n_s.shape, 0) // heads
            key = lax.broadcasted_iota(jnp.int32, n_s.shape, 1)
            seen = (key >= b * steps) & (key <= row) & (lax.rem(me, 2 * SIDE) == 0)
            n_s = jnp.where(seen, n_s, NEG)
            m = jnp.maximum(m, jnp.max(n_s, axis=1, keepdims=True))
        p = jnp.exp2((s - m) * coef)
        total = jnp.sum(p, axis=1, keepdims=True)
        o = jnp.dot(p.astype(BF16), vt[b], preferred_element_type=F32)
        if near:
            n_p = jnp.where(seen, jnp.exp2((n_s - m) * coef), 0.0)
            total = total + jnp.sum(n_p, axis=1, keepdims=True)
            o = o + jnp.dot(n_p.astype(BF16), nl[:, :latent], preferred_element_type=F32)
        return o.astype(BF16), m * coef, total

    def pair_of(p):
        return lax.rem(y + p, SIDE)

    head_of = lax.broadcasted_iota(jnp.int32, (per, LANES), 0) & (heads - 1)
    lane_of = lax.broadcasted_iota(jnp.int32, (per, LANES), 1)
    lane = lax.broadcasted_iota(jnp.int32, (8, LANES), 1)

    def spread(column):
        one = jnp.where(head_of == lane_of, column, 0.0).reshape(steps, heads, LANES)
        return jnp.sum(one, axis=1)

    def work(p, u, near):
        b = 2 * pair_of(p) + u
        o, m, total = attend(b, near)
        ot[p, u * per : (u + 1) * per, :] = o
        tops[p, u * steps : (u + 1) * steps, :] = spread(m)
        sums[p, u * steps : (u + 1) * steps, :] = spread(total)

    owners = [(2, 0), (2, 1), (1, 0), (1, 1), (3, 0), (3, 1), (0, 1)]

    def to_owner(p, dy, dc):
        to_y = lax.rem(y + dy, SIDE)
        to_core = lax.rem(core + dc, 2)
        to = to_y * (2 * SIDE) + pair_of(p) * 2 + to_core
        k = (p * SIDE + dy) * 2 + dc
        return (
            pltpu.make_async_remote_copy(
                src_ref=st.at[p, to_core, to_y],
                dst_ref=rb.at[me],
                send_sem=r_send.at[k],
                recv_sem=r_recv.at[me],
                device_id={"ctx": to},
                device_id_type=MESH,
            ),
            pltpu.make_async_remote_copy(
                src_ref=stl.at[p, to_core],
                dst_ref=rbl.at[me],
                send_sem=r_send.at[rows + k],
                recv_sem=r_recv.at[rows + me],
                device_id={"ctx": to},
                device_id_type=MESH,
            ),
        )

    def project(pairs):
        turned = []
        for p in pairs:
            t = jnp.dot(perm[...], ot[p], preferred_element_type=F32)
            turned.append(t.astype(BF16))
            a, b = tops[p], sums[p]
            stl[p, 0] = jnp.where(lane < 16, a, pltpu.roll(b, 16, 1))
            stl[p, 1] = jnp.where(lane < 16, pltpu.roll(a, LANES - 16, 1), b)
        blocks = [[] for _ in pairs]
        for g in range(heads // 8):
            w = jnp.concatenate([vu[g * 8 + k] for k in range(8)], axis=1)
            x = jnp.concatenate([t[g * 64 : g * 64 + 64] for t in turned], axis=0)
            r = jnp.dot(x, w, preferred_element_type=F32)
            for i in range(len(pairs)):
                part = r[i * 64 : i * 64 + 64]
                blocks[i].append(
                    jnp.concatenate(
                        [part[k * 8 : k * 8 + 8, k * LANES : (k + 1) * LANES] for k in range(8)],
                        axis=1,
                    )
                )
        for i, p in enumerate(pairs):
            for c in range(2):
                half_state = jnp.concatenate(blocks[i][2 * c : 2 * c + 2], axis=0).astype(BF16)
                for k in range(SIDE):
                    st[p, c, k] = half_state[:, k * 256 : k * 256 + 256]
            mine = pair_of(p) == z

            @pl.when(mine)
            def _(p=p):
                rb[me] = st[p, core, y]
                rbl[me] = stl[p, core]

            @pl.when(jnp.logical_not(mine))
            def _(p=p):
                for copy in to_owner(p, 0, 0):
                    copy.start()

            for dy, dc in owners:
                for copy in to_owner(p, dy, dc):
                    copy.start()

    get_ku.wait()
    get_nl.wait()
    get_vu.wait()
    get_op.wait()
    absorb([y])
    for i, (dy, dz) in enumerate(across[::-1]):
        got_q(at(dy, dz))
        q_sends[19 + i].start()
    work(0, 0, True)
    for dy in range(1, SIDE):
        for dz in range(SIDE):
            got_q(at(dy, dz, 1))
    absorb([pair_of(p) for p in range(1, SIDE)])
    work(0, 1, True)
    @pl.loop(1, SIDE - 1)
    def _(p):
        work(p, 0, False)
        work(p, 1, False)

    project(range(SIDE - 1))
    work(SIDE - 1, 0, False)
    work(SIDE - 1, 1, False)
    project([SIDE - 1])

    def from_peer(source):
        return (
            pltpu.make_async_remote_copy(
                src_ref=st.at[0, 0, 0],
                dst_ref=rb.at[source],
                send_sem=r_send.at[0],
                recv_sem=r_recv.at[source],
                device_id={"ctx": sibling},
                device_id_type=MESH,
            ),
            pltpu.make_async_remote_copy(
                src_ref=stl.at[0, 0],
                dst_ref=rbl.at[source],
                send_sem=r_send.at[0],
                recv_sem=r_recv.at[rows + source],
                device_id={"ctx": sibling},
                device_id_type=MESH,
            ),
        )

    for d in everyone:
        for copy in from_peer(at(*d)):
            copy.wait_recv()

    stats = rbl[...]
    top = jnp.max(stats, axis=0)
    w = jnp.exp2(stats - top[None])
    totals = pltpu.roll(stats.reshape(rows * 8, LANES), LANES - 16, 1).reshape(rows, 8, LANES)
    w = w / jnp.sum(w * totals, axis=0)[None]
    w = pltpu.roll(w.reshape(rows * 8, LANES), lax.rem(LANES - 2 * y, LANES), 1)
    acc = jnp.zeros((16, 256), F32)
    for s in range(rows):
        f = w[s * 8 : s * 8 + 8]
        f = [jnp.broadcast_to(f[:, i : i + 1], (8, LANES)) for i in (0, 1, 8, 9)]
        f = jnp.concatenate(
            [jnp.concatenate(f[:2], axis=1), jnp.concatenate(f[2:], axis=1)], axis=0
        )
        acc = acc + rb[s].astype(F32) * f
    ho[...] = acc.astype(BF16)
    hg[core, z, y] = ho[...]

    def send_h(to, source):
        return pltpu.make_async_remote_copy(
            src_ref=ho,
            dst_ref=hg.at[
                lax.rem(source, 2), lax.rem(source // 2, SIDE), source // (2 * SIDE)
            ],
            send_sem=h_send.at[to],
            recv_sem=h_recv.at[source],
            device_id={"ctx": to},
            device_id_type=MESH,
        )

    for d in everyone:
        send_h(at(*d), me).start()
    for d in everyone:
        send_h(at(*d), at(*d)).wait_recv()

    total = jnp.zeros((rows, out.shape[1]), F32)
    for c in range(2):
        for i in range(SIDE):
            x = [hg[c, pair, i].astype(F32) for pair in range(SIDE)]
            for u in range(2):
                lhs = jnp.concatenate([a[u * 8 : u * 8 + 8] for a in x], axis=0).astype(BF16)
                first = (c * 16 + u * 8 + i * 2) * LANES
                total = total + lax.dot_general(
                    lhs, op[:, first : first + 256], contract, preferred_element_type=F32
                )
    xb[group] = total.astype(BF16)

    def send_x(to, slot):
        return pltpu.make_async_remote_copy(
            src_ref=xb.at[group],
            dst_ref=xb.at[slot],
            send_sem=x_send.at[to],
            recv_sem=x_recv.at[slot],
            device_id={"heads": to},
            device_id_type=MESH,
        )

    for i in range(1, groups):
        send_x(lax.rem(group + i, groups), group).start()
    for i in range(1, groups):
        other = lax.rem(group + i, groups)
        send_x(other, other).wait_recv()
    result = xb[0].astype(F32)
    for g in range(1, groups):
        result = result + xb[g].astype(F32)
    out[...] = result.astype(out.dtype)

    for copy in q_sends:
        copy.wait_send()
    for p in range(SIDE):

        @pl.when(pair_of(p) != z)
        def _(p=p):
            for copy in to_owner(p, 0, 0):
                copy.wait_send()

        for dy, dc in owners:
            for copy in to_owner(p, dy, dc):
                copy.wait_send()
    for d in everyone:
        send_h(at(*d), me).wait_send()
    for i in range(1, groups):
        send_x(lax.rem(group + i, groups), group).wait_send()


def local(groups, queries, cache, fresh, lengths, key_up, value_up, out_proj):
    cache = jnp.swapaxes(cache, 1, 2)
    out_proj = jnp.swapaxes(out_proj, 0, 1)
    heads, nope, latent = key_up.shape
    reqs, width, keys = cache.shape
    rows = fresh.shape[0]
    vdim = value_up.shape[2]
    columns = out_proj.shape[0]
    per = rows // reqs * heads
    hbm = pl.BlockSpec(memory_space=pl.ANY)
    dma = pltpu.SemaphoreType.DMA
    return pl.pallas_call(
        functools.partial(kernel, groups),
        out_shape=jax.ShapeDtypeStruct((rows, columns), BF16),
        in_specs=[hbm] * 7,
        out_specs=pl.BlockSpec(memory_space=pltpu.VMEM),
        scratch_shapes=[
            pltpu.VMEM((reqs, width, keys), BF16),
            pltpu.VMEM((reqs, keys, latent), BF16),
            pltpu.VMEM((heads, nope, latent), BF16),
            pltpu.VMEM((heads, latent, vdim), BF16),
            pltpu.VMEM((columns, heads * vdim), BF16),
            pltpu.VMEM((rows, width), BF16),
            pltpu.SMEM((reqs,), jnp.int32),
            pltpu.VMEM((heads, queries.shape[2]), BF16),
            pltpu.VMEM((rows, heads + heads // 2, LANES), BF16),
            pltpu.VMEM((rows, heads, width), BF16),
            pltpu.VMEM((2 * per, 2 * per), BF16),
            pltpu.VMEM((SIDE, 2 * per, latent), BF16),
            pltpu.VMEM((SIDE, 8, LANES), F32),
            pltpu.VMEM((SIDE, 8, LANES), F32),
            pltpu.VMEM((SIDE, 2, SIDE, 16, 256), BF16),
            pltpu.VMEM((SIDE, 2, 8, LANES), F32),
            pltpu.VMEM((rows, 16, 256), BF16),
            pltpu.VMEM((rows, 8, LANES), F32),
            pltpu.VMEM((16, 256), BF16),
            pltpu.VMEM((2, SIDE, SIDE, 16, 256), BF16),
            pltpu.VMEM((groups, rows, columns), BF16),
            dma((reqs,)),
            dma((6,)),
            dma((31,)),
            dma((rows,)),
            dma((2 * rows,)),
            dma((2 * rows,)),
            dma((rows,)),
            dma((rows,)),
            dma((groups,)),
            dma((groups,)),
        ],
        compiler_params=pltpu.CompilerParams(
            collective_id=0, has_side_effects=True, vmem_limit_bytes=56 * 1024 * 1024
        ),
        cost_estimate=pl.CostEstimate(
            flops=4 * 10**9, bytes_accessed=25 * 10**6, transcendentals=2 * 10**6
        ),
        name="mla_decode",
    )(queries, cache, fresh, lengths, key_up, value_up, out_proj)


def solution(mesh):
    in_specs = (
        P("ctx", "heads", None),
        P(None, "ctx", None),
        P(),
        P(),
        P("heads", None, None),
        P("heads", None, None),
        P("heads", "ctx"),
    )
    body = functools.partial(local, mesh.shape["heads"])
    return jax.shard_map(
        body, mesh=mesh, in_specs=in_specs, out_specs=P(None, "ctx"), check_vma=False
    )
```

```python
import functools
import math

import jax
import jax.numpy as jnp
from jax import lax
from jax.experimental import pallas as pl
from jax.experimental.pallas import tpu as pltpu
from jax.sharding import PartitionSpec as P

NEG = -3e38
MESH = pl.DeviceIdType.MESH
F32 = jnp.float32
BF16 = jnp.bfloat16
SIDE = 4
LANES = 128


def kernel(
    groups,
    queries,
    cache,
    fresh,
    lengths_in,
    key_up,
    value_up,
    out_proj,
    out,
    kc,
    vt,
    ku,
    vu,
    op,
    opt,
    nl,
    lengths,
    qown,
    qg,
    qfull,
    perm,
    ot,
    tops,
    sums,
    st,
    stl,
    rb,
    rbl,
    ho,
    hg,
    xb,
    cache_sem,
    local_sem,
    q_send,
    q_recv,
    r_send,
    r_recv,
    h_send,
    h_recv,
    x_send,
    x_recv,
):
    me = lax.axis_index("ctx")
    group = lax.axis_index("heads")
    core = lax.rem(me, 2)
    z = lax.rem(me // 2, SIDE)
    y = me // (2 * SIDE)
    rows = fresh.shape[0]
    heads, nope, latent = key_up.shape
    reqs, width, keys = cache.shape
    steps = rows // reqs
    per = steps * heads
    coef = math.log2(math.e) / math.sqrt(queries.shape[2])
    contract = (((1,), (1,)), ((), ()))

    def at(dy, dz, dc=0):
        return (
            lax.rem(y + dy, SIDE) * (2 * SIDE) + lax.rem(z + dz, SIDE) * 2 + lax.rem(core + dc, 2)
        )

    sibling = at(0, 0, 1)
    others = [(dy, dz) for dy in range(SIDE) for dz in range(SIDE) if dy or dz]
    hops = (0, 1, 2, 1)
    everyone = [(dy, dz, dc) for dy, dz in [(0, 0)] + others for dc in range(2) if dy or dz or dc]
    everyone.sort(key=lambda d: -hops[d[0]] - hops[d[1]])

    own_q = pltpu.make_async_copy(queries.at[0], qown, local_sem.at[0])
    get_ku = pltpu.make_async_copy(key_up, ku, local_sem.at[1])
    get_vu = pltpu.make_async_copy(value_up, vu, local_sem.at[2])
    get_op = pltpu.make_async_copy(out_proj, op, local_sem.at[3])
    get_nl = pltpu.make_async_copy(fresh, nl, local_sem.at[4])
    get_lengths = pltpu.make_async_copy(lengths_in, lengths, local_sem.at[5])

    def get_cache(b):
        return pltpu.make_async_copy(cache.at[b], kc.at[b], cache_sem.at[b])

    own_q.start()
    get_nl.start()
    get_lengths.start()
    get_ku.start()
    for u in range(2):
        get_cache(2 * y + u).start()

    @pl.loop(2, reqs)
    def _(i):
        get_cache(lax.rem(2 * y + i, reqs)).start()

    get_vu.start()
    get_op.start()

    barrier = pltpu.get_barrier_semaphore()
    peers = [sibling] + [at(dy, dz) for dy, dz in others]
    for to in peers:
        pl.semaphore_signal(barrier, inc=1, device_id={"ctx": to}, device_id_type=MESH)
    for i in range(1, groups):
        pl.semaphore_signal(
            barrier, inc=1, device_id={"heads": lax.rem(group + i, groups)}, device_id_type=MESH
        )
    to_row = lax.broadcasted_iota(jnp.int32, (2 * per, 2 * per), 0)
    of_row = lax.broadcasted_iota(jnp.int32, (2 * per, 2 * per), 1)
    perm[...] = jnp.where(
        of_row == (to_row & (2 * steps - 1)) * heads + to_row // (2 * steps), 1.0, 0.0
    ).astype(BF16)
    own_q.wait()
    rope = width - latent
    half = heads // 2
    qg[me, :heads] = qown[:, :nope]
    qg[me, heads:] = jnp.concatenate([qown[:half, nope:], qown[half:, nope:]], axis=1)
    get_lengths.wait()
    pl.semaphore_wait(barrier, len(peers) + groups - 1)

    def send_q(to, row, k):
        return pltpu.make_async_remote_copy(
            src_ref=qg.at[row],
            dst_ref=qg.at[row],
            send_sem=q_send.at[k],
            recv_sem=q_recv.at[row],
            device_id={"ctx": to},
            device_id_type=MESH,
        )

    along_z = [(0, 1), (0, 3), (0, 2)]
    across = [(2, 2), (2, 1), (2, 3), (1, 2), (3, 2), (1, 1), (1, 3), (3, 1), (3, 3)]
    across += [(2, 0), (1, 0), (3, 0)]
    q_sends = [(sibling, me)] + [(at(dy, dz), me) for dy, dz in along_z + across]
    q_sends += [(sibling, at(dy, dz)) for dy, dz in along_z + across[::-1]]
    q_sends = [send_q(to, row, k) for k, (to, row) in enumerate(q_sends)]

    def got_q(row):
        send_q(sibling, row, 0).wait_recv()

    for k in range(16):
        q_sends[k].start()

    @pl.loop(0, reqs)
    def _(i):
        b = lax.rem(2 * y + i, reqs)
        get_cache(b).wait()
        for c in range(latent // LANES):
            vt[b, :, c * LANES : (c + 1) * LANES] = jnp.transpose(
                kc[b, c * LANES : (c + 1) * LANES, :]
            )

    for i, (dy, dz) in enumerate(along_z):
        got_q(at(dy, dz))
        q_sends[16 + i].start()
    for dz in range(SIDE):
        got_q(at(0, dz, 1))

    def absorb(pairs):
        starts = [pl.multiple_of(j * 8, 8) for j in pairs]
        many = 8 * len(pairs)
        which = lax.broadcasted_iota(jnp.int32, (many, 8, LANES), 1)
        for two in range(heads // 16):
            span = slice(two * 16, two * 16 + 16)
            x = jnp.concatenate([qg[pl.ds(s, 8), span, :] for s in starts], axis=0).astype(F32)
            halves = []
            for u in range(2):
                part = x[:, u * 8 : u * 8 + 8, :]
                wide = jnp.concatenate(
                    [
                        jnp.where(which == k, part, 0.0).reshape(many * 8, LANES).astype(BF16)
                        for k in range(8)
                    ],
                    axis=1,
                )
                first = two * 16 + u * 8
                w = ku[first : first + 8].reshape(8 * nope, latent)
                halves.append(
                    jnp.dot(wide, w, preferred_element_type=F32).reshape(many, 8, latent)
                )
            lat = jnp.concatenate(halves, axis=1).astype(BF16)
            for i, s in enumerate(starts):
                qfull[pl.ds(s, 8), span, :latent] = lat[i * 8 : i * 8 + 8]
        for s in starts:
            qfull[pl.ds(s, 8), :half, latent:] = qg[pl.ds(s, 8), heads:, :rope]
            qfull[pl.ds(s, 8), half:, latent:] = qg[pl.ds(s, 8), heads:, rope:]

    position = me * keys + lax.broadcasted_iota(jnp.int32, (1, keys), 1)

    def attend(b, near):
        q = qfull[pl.ds(b * steps, steps)].reshape(per, width)
        s = jnp.dot(q, kc[b], preferred_element_type=F32)
        s = jnp.where(position < lengths[b], s, NEG)
        m = jnp.max(s, axis=1, keepdims=True)
        if near:
            n_s = lax.dot_general(q, nl[...], contract, preferred_element_type=F32)
            row = b * steps + lax.broadcasted_iota(jnp.int32, n_s.shape, 0) // heads
            key = lax.broadcasted_iota(jnp.int32, n_s.shape, 1)
            seen = (key >= b * steps) & (key <= row) & (lax.rem(me, 2 * SIDE) == 0)
            n_s = jnp.where(seen, n_s, NEG)
            m = jnp.maximum(m, jnp.max(n_s, axis=1, keepdims=True))
        p = jnp.exp2((s - m) * coef)
        total = jnp.sum(p, axis=1, keepdims=True)
        o = jnp.dot(p.astype(BF16), vt[b], preferred_element_type=F32)
        if near:
            n_p = jnp.where(seen, jnp.exp2((n_s - m) * coef), 0.0)
            total = total + jnp.sum(n_p, axis=1, keepdims=True)
            o = o + jnp.dot(n_p.astype(BF16), nl[:, :latent], preferred_element_type=F32)
        return o.astype(BF16), m * coef, total

    def pair_of(p):
        return lax.rem(y + p, SIDE)

    head_of = lax.broadcasted_iota(jnp.int32, (per, LANES), 0) & (heads - 1)
    lane_of = lax.broadcasted_iota(jnp.int32, (per, LANES), 1)
    lane = lax.broadcasted_iota(jnp.int32, (8, LANES), 1)

    def spread(column):
        one = jnp.where(head_of == lane_of, column, 0.0).reshape(steps, heads, LANES)
        return jnp.sum(one, axis=1)

    def work(p, u, near):
        b = 2 * pair_of(p) + u
        o, m, total = attend(b, near)
        ot[p, u * per : (u + 1) * per, :] = o
        tops[p, u * steps : (u + 1) * steps, :] = spread(m)
        sums[p, u * steps : (u + 1) * steps, :] = spread(total)

    owners = [(2, 0), (2, 1), (1, 0), (1, 1), (3, 0), (3, 1), (0, 1)]

    def to_owner(p, dy, dc):
        to_y = lax.rem(y + dy, SIDE)
        to_core = lax.rem(core + dc, 2)
        to = to_y * (2 * SIDE) + pair_of(p) * 2 + to_core
        k = (p * SIDE + dy) * 2 + dc
        return (
            pltpu.make_async_remote_copy(
                src_ref=st.at[p, to_core, to_y],
                dst_ref=rb.at[me],
                send_sem=r_send.at[k],
                recv_sem=r_recv.at[me],
                device_id={"ctx": to},
                device_id_type=MESH,
            ),
            pltpu.make_async_remote_copy(
                src_ref=stl.at[p, to_core],
                dst_ref=rbl.at[me],
                send_sem=r_send.at[rows + k],
                recv_sem=r_recv.at[rows + me],
                device_id={"ctx": to},
                device_id_type=MESH,
            ),
        )

    def project(pairs):
        turned = []
        for p in pairs:
            t = jnp.dot(perm[...], ot[p], preferred_element_type=F32)
            turned.append(t.astype(BF16))
            a, b = tops[p], sums[p]
            stl[p, 0] = jnp.where(lane < 16, a, pltpu.roll(b, 16, 1))
            stl[p, 1] = jnp.where(lane < 16, pltpu.roll(a, LANES - 16, 1), b)
        blocks = [[] for _ in pairs]
        for g in range(heads // 8):
            w = jnp.concatenate([vu[g * 8 + k] for k in range(8)], axis=1)
            x = jnp.concatenate([t[g * 64 : g * 64 + 64] for t in turned], axis=0)
            r = jnp.dot(x, w, preferred_element_type=F32)
            for i in range(len(pairs)):
                part = r[i * 64 : i * 64 + 64]
                blocks[i].append(
                    jnp.concatenate(
                        [part[k * 8 : k * 8 + 8, k * LANES : (k + 1) * LANES] for k in range(8)],
                        axis=1,
                    )
                )
        for i, p in enumerate(pairs):
            for c in range(2):
                half_state = jnp.concatenate(blocks[i][2 * c : 2 * c + 2], axis=0).astype(BF16)
                for k in range(SIDE):
                    st[p, c, k] = half_state[:, k * 256 : k * 256 + 256]
            mine = pair_of(p) == z

            @pl.when(mine)
            def _(p=p):
                rb[me] = st[p, core, y]
                rbl[me] = stl[p, core]

            @pl.when(jnp.logical_not(mine))
            def _(p=p):
                for copy in to_owner(p, 0, 0):
                    copy.start()

            for dy, dc in owners:
                for copy in to_owner(p, dy, dc):
                    copy.start()

    get_ku.wait()
    get_nl.wait()
    get_vu.wait()
    get_op.wait()
    absorb([y])
    for i, (dy, dz) in enumerate(across[::-1]):
        got_q(at(dy, dz))
        q_sends[19 + i].start()
    work(0, 0, True)
    for dy in range(1, SIDE):
        for dz in range(SIDE):
            got_q(at(dy, dz, 1))
    absorb([pair_of(p) for p in range(1, SIDE)])
    work(0, 1, True)
    @pl.loop(1, SIDE - 1)
    def _(p):
        work(p, 0, False)
        work(p, 1, False)

    project(range(SIDE - 1))
    work(SIDE - 1, 0, False)
    work(SIDE - 1, 1, False)
    project([SIDE - 1])

    def from_peer(source):
        return (
            pltpu.make_async_remote_copy(
                src_ref=st.at[0, 0, 0],
                dst_ref=rb.at[source],
                send_sem=r_send.at[0],
                recv_sem=r_recv.at[source],
                device_id={"ctx": sibling},
                device_id_type=MESH,
            ),
            pltpu.make_async_remote_copy(
                src_ref=stl.at[0, 0],
                dst_ref=rbl.at[source],
                send_sem=r_send.at[0],
                recv_sem=r_recv.at[rows + source],
                device_id={"ctx": sibling},
                device_id_type=MESH,
            ),
        )

    @pl.loop(0, heads * LANES // 512)
    def _(i):
        span = pl.ds(pl.multiple_of(i * 512, 512), 512)
        opt[span, :] = jnp.transpose(op[:, span])

    for copy in q_sends:
        copy.wait_send()
    for d in everyone:
        for copy in from_peer(at(*d)):
            copy.wait_recv()

    stats = rbl[...]
    top = jnp.max(stats, axis=0)
    w = jnp.exp2(stats - top[None])
    totals = pltpu.roll(stats.reshape(rows * 8, LANES), LANES - 16, 1).reshape(rows, 8, LANES)
    w = w / jnp.sum(w * totals, axis=0)[None]
    w = pltpu.roll(w.reshape(rows * 8, LANES), lax.rem(LANES - 2 * y, LANES), 1)
    acc = jnp.zeros((16, 256), F32)
    for s in range(rows):
        f = w[s * 8 : s * 8 + 8]
        f = [jnp.broadcast_to(f[:, i : i + 1], (8, LANES)) for i in (0, 1, 8, 9)]
        f = jnp.concatenate(
            [jnp.concatenate(f[:2], axis=1), jnp.concatenate(f[2:], axis=1)], axis=0
        )
        acc = acc + rb[s].astype(F32) * f
    ho[...] = acc.astype(BF16)
    hg[core, z, y] = ho[...]

    def send_h(to, source):
        return pltpu.make_async_remote_copy(
            src_ref=ho,
            dst_ref=hg.at[
                lax.rem(source, 2), lax.rem(source // 2, SIDE), source // (2 * SIDE)
            ],
            send_sem=h_send.at[to],
            recv_sem=h_recv.at[source],
            device_id={"ctx": to},
            device_id_type=MESH,
        )

    for d in everyone:
        send_h(at(*d), me).start()
    for p in range(SIDE):

        @pl.when(pair_of(p) != z)
        def _(p=p):
            for copy in to_owner(p, 0, 0):
                copy.wait_send()

        for dy, dc in owners:
            for copy in to_owner(p, dy, dc):
                copy.wait_send()
    for d in everyone:
        send_h(at(*d), at(*d)).wait_recv()

    total = jnp.zeros((rows, out.shape[1]), F32)
    for c in range(2):
        for i in range(SIDE):
            x = [hg[c, pair, i].astype(F32) for pair in range(SIDE)]
            for u in range(2):
                lhs = jnp.concatenate([a[u * 8 : u * 8 + 8] for a in x], axis=0).astype(BF16)
                first = (c * 16 + u * 8 + i * 2) * LANES
                total = total + jnp.dot(
                    lhs, opt[first : first + 256, :], preferred_element_type=F32
                )
    xb[group] = total.astype(BF16)

    def send_x(to, slot):
        return pltpu.make_async_remote_copy(
            src_ref=xb.at[group],
            dst_ref=xb.at[slot],
            send_sem=x_send.at[to],
            recv_sem=x_recv.at[slot],
            device_id={"heads": to},
            device_id_type=MESH,
        )

    for i in range(1, groups):
        send_x(lax.rem(group + i, groups), group).start()
    for d in everyone:
        send_h(at(*d), me).wait_send()
    for i in range(1, groups):
        other = lax.rem(group + i, groups)
        send_x(other, other).wait_recv()
    result = xb[0].astype(F32)
    for g in range(1, groups):
        result = result + xb[g].astype(F32)
    out[...] = result.astype(out.dtype)

    for i in range(1, groups):
        send_x(lax.rem(group + i, groups), group).wait_send()


def local(groups, queries, cache, fresh, lengths, key_up, value_up, out_proj):
    cache = jnp.swapaxes(cache, 1, 2)
    out_proj = jnp.swapaxes(out_proj, 0, 1)
    heads, nope, latent = key_up.shape
    reqs, width, keys = cache.shape
    rows = fresh.shape[0]
    vdim = value_up.shape[2]
    columns = out_proj.shape[0]
    per = rows // reqs * heads
    hbm = pl.BlockSpec(memory_space=pl.ANY)
    dma = pltpu.SemaphoreType.DMA
    return pl.pallas_call(
        functools.partial(kernel, groups),
        out_shape=jax.ShapeDtypeStruct((rows, columns), BF16),
        in_specs=[hbm] * 7,
        out_specs=pl.BlockSpec(memory_space=pltpu.VMEM),
        scratch_shapes=[
            pltpu.VMEM((reqs, width, keys), BF16),
            pltpu.VMEM((reqs, keys, latent), BF16),
            pltpu.VMEM((heads, nope, latent), BF16),
            pltpu.VMEM((heads, latent, vdim), BF16),
            pltpu.VMEM((columns, heads * vdim), BF16),
            pltpu.VMEM((heads * vdim, columns), BF16),
            pltpu.VMEM((rows, width), BF16),
            pltpu.SMEM((reqs,), jnp.int32),
            pltpu.VMEM((heads, queries.shape[2]), BF16),
            pltpu.VMEM((rows, heads + heads // 2, LANES), BF16),
            pltpu.VMEM((rows, heads, width), BF16),
            pltpu.VMEM((2 * per, 2 * per), BF16),
            pltpu.VMEM((SIDE, 2 * per, latent), BF16),
            pltpu.VMEM((SIDE, 8, LANES), F32),
            pltpu.VMEM((SIDE, 8, LANES), F32),
            pltpu.VMEM((SIDE, 2, SIDE, 16, 256), BF16),
            pltpu.VMEM((SIDE, 2, 8, LANES), F32),
            pltpu.VMEM((rows, 16, 256), BF16),
            pltpu.VMEM((rows, 8, LANES), F32),
            pltpu.VMEM((16, 256), BF16),
            pltpu.VMEM((2, SIDE, SIDE, 16, 256), BF16),
            pltpu.VMEM((groups, rows, columns), BF16),
            dma((reqs,)),
            dma((6,)),
            dma((31,)),
            dma((rows,)),
            dma((2 * rows,)),
            dma((2 * rows,)),
            dma((rows,)),
            dma((rows,)),
            dma((groups,)),
            dma((groups,)),
        ],
        compiler_params=pltpu.CompilerParams(
            collective_id=0, has_side_effects=True, vmem_limit_bytes=56 * 1024 * 1024
        ),
        cost_estimate=pl.CostEstimate(
            flops=4 * 10**9, bytes_accessed=25 * 10**6, transcendentals=2 * 10**6
        ),
        name="mla_decode",
    )(queries, cache, fresh, lengths, key_up, value_up, out_proj)


def solution(mesh):
    in_specs = (
        P("ctx", "heads", None),
        P(None, "ctx", None),
        P(),
        P(),
        P("heads", None, None),
        P("heads", None, None),
        P("heads", "ctx"),
    )
    body = functools.partial(local, mesh.shape["heads"])
    return jax.shard_map(
        body, mesh=mesh, in_specs=in_specs, out_specs=P(None, "ctx"), check_vma=False
    )
```

```python
import functools
import math

import jax
import jax.numpy as jnp
from jax import lax
from jax.experimental import pallas as pl
from jax.experimental.pallas import tpu as pltpu
from jax.sharding import PartitionSpec as P

NEG = -3e38
MESH = pl.DeviceIdType.MESH
F32 = jnp.float32
BF16 = jnp.bfloat16
SIDE = 4
LANES = 128


def kernel(
    groups,
    queries,
    cache,
    fresh,
    lengths_in,
    key_up,
    value_up,
    out_proj,
    out,
    kc,
    vt,
    ku,
    vu,
    op,
    opt,
    nl,
    lengths,
    qown,
    qg,
    qfull,
    perm,
    ot,
    tops,
    sums,
    st,
    stl,
    rb,
    rbl,
    ho,
    hg,
    xb,
    cache_sem,
    local_sem,
    q_send,
    q_recv,
    r_send,
    r_recv,
    h_send,
    h_recv,
    x_send,
    x_recv,
):
    me = lax.axis_index("ctx")
    group = lax.axis_index("heads")
    core = lax.rem(me, 2)
    z = lax.rem(me // 2, SIDE)
    y = me // (2 * SIDE)
    rows = fresh.shape[0]
    heads, nope, latent = key_up.shape
    reqs, width, keys = cache.shape
    steps = rows // reqs
    per = steps * heads
    coef = math.log2(math.e) / math.sqrt(queries.shape[2])
    contract = (((1,), (1,)), ((), ()))

    def at(dy, dz, dc=0):
        return (
            lax.rem(y + dy, SIDE) * (2 * SIDE) + lax.rem(z + dz, SIDE) * 2 + lax.rem(core + dc, 2)
        )

    sibling = at(0, 0, 1)
    others = [(dy, dz) for dy in range(SIDE) for dz in range(SIDE) if dy or dz]
    hops = (0, 1, 2, 1)
    everyone = [(dy, dz, dc) for dy, dz in [(0, 0)] + others for dc in range(2) if dy or dz or dc]
    everyone.sort(key=lambda d: -hops[d[0]] - hops[d[1]])

    own_q = pltpu.make_async_copy(queries.at[0], qown, local_sem.at[0])
    get_ku = pltpu.make_async_copy(key_up, ku, local_sem.at[1])
    get_vu = pltpu.make_async_copy(value_up, vu, local_sem.at[2])
    get_op = pltpu.make_async_copy(out_proj, op, local_sem.at[3])
    get_nl = pltpu.make_async_copy(fresh, nl, local_sem.at[4])
    get_lengths = pltpu.make_async_copy(lengths_in, lengths, local_sem.at[5])

    def get_cache(b):
        return pltpu.make_async_copy(cache.at[b], kc.at[b], cache_sem.at[b])

    own_q.start()
    get_nl.start()
    get_lengths.start()
    get_ku.start()
    for u in range(2):
        get_cache(2 * y + u).start()

    @pl.loop(2, reqs)
    def _(i):
        get_cache(lax.rem(2 * y + i, reqs)).start()

    get_vu.start()
    get_op.start()

    barrier = pltpu.get_barrier_semaphore()
    peers = [sibling] + [at(dy, dz) for dy, dz in others]
    for to in peers:
        pl.semaphore_signal(barrier, inc=1, device_id={"ctx": to}, device_id_type=MESH)
    for i in range(1, groups):
        pl.semaphore_signal(
            barrier, inc=1, device_id={"heads": lax.rem(group + i, groups)}, device_id_type=MESH
        )
    to_row = lax.broadcasted_iota(jnp.int32, (2 * per, 2 * per), 0)
    of_row = lax.broadcasted_iota(jnp.int32, (2 * per, 2 * per), 1)
    perm[...] = jnp.where(
        of_row == (to_row & (2 * steps - 1)) * heads + to_row // (2 * steps), 1.0, 0.0
    ).astype(BF16)
    own_q.wait()
    rope = width - latent
    half = heads // 2
    qg[me, :heads] = qown[:, :nope]
    qg[me, heads:] = jnp.concatenate([qown[:half, nope:], qown[half:, nope:]], axis=1)
    get_lengths.wait()
    pl.semaphore_wait(barrier, len(peers) + groups - 1)

    def send_q(to, row, k):
        return pltpu.make_async_remote_copy(
            src_ref=qg.at[row],
            dst_ref=qg.at[row],
            send_sem=q_send.at[k],
            recv_sem=q_recv.at[row],
            device_id={"ctx": to},
            device_id_type=MESH,
        )

    along_z = [(0, 1), (0, 3), (0, 2)]
    across = [(2, 2), (2, 1), (2, 3), (1, 2), (3, 2), (1, 1), (1, 3), (3, 1), (3, 3)]
    across += [(2, 0), (1, 0), (3, 0)]
    q_sends = [(sibling, me)] + [(at(dy, dz), me) for dy, dz in along_z + across]
    q_sends += [(sibling, at(dy, dz)) for dy, dz in along_z + across[::-1]]
    q_sends = [send_q(to, row, k) for k, (to, row) in enumerate(q_sends)]

    def got_q(row):
        send_q(sibling, row, 0).wait_recv()

    for k in range(16):
        q_sends[k].start()

    @pl.loop(0, reqs)
    def _(i):
        b = lax.rem(2 * y + i, reqs)
        get_cache(b).wait()
        for c in range(latent // LANES):
            vt[b, :, c * LANES : (c + 1) * LANES] = jnp.transpose(
                kc[b, c * LANES : (c + 1) * LANES, :]
            )

    for i, (dy, dz) in enumerate(along_z):
        got_q(at(dy, dz))
        q_sends[16 + i].start()
    for dz in range(SIDE):
        got_q(at(0, dz, 1))

    def absorb(pairs):
        starts = [pl.multiple_of(j * 8, 8) for j in pairs]
        many = 8 * len(pairs)
        which = lax.broadcasted_iota(jnp.int32, (many, 8, LANES), 1)
        for two in range(heads // 16):
            span = slice(two * 16, two * 16 + 16)
            x = jnp.concatenate([qg[pl.ds(s, 8), span, :] for s in starts], axis=0).astype(F32)
            halves = []
            for u in range(2):
                part = x[:, u * 8 : u * 8 + 8, :]
                wide = jnp.concatenate(
                    [
                        jnp.where(which == k, part, 0.0).reshape(many * 8, LANES).astype(BF16)
                        for k in range(8)
                    ],
                    axis=1,
                )
                first = two * 16 + u * 8
                w = ku[first : first + 8].reshape(8 * nope, latent)
                halves.append(
                    jnp.dot(wide, w, preferred_element_type=F32).reshape(many, 8, latent)
                )
            lat = jnp.concatenate(halves, axis=1).astype(BF16)
            for i, s in enumerate(starts):
                qfull[pl.ds(s, 8), span, :latent] = lat[i * 8 : i * 8 + 8]
        for s in starts:
            qfull[pl.ds(s, 8), :half, latent:] = qg[pl.ds(s, 8), heads:, :rope]
            qfull[pl.ds(s, 8), half:, latent:] = qg[pl.ds(s, 8), heads:, rope:]

    position = me * keys + lax.broadcasted_iota(jnp.int32, (1, keys), 1)

    def attend(b, near):
        q = qfull[pl.ds(b * steps, steps)].reshape(per, width)
        s = jnp.dot(q, kc[b], preferred_element_type=F32)
        s = jnp.where(position < lengths[b], s, NEG)
        m = jnp.max(s, axis=1, keepdims=True)
        if near:
            n_s = lax.dot_general(q, nl[...], contract, preferred_element_type=F32)
            row = b * steps + lax.broadcasted_iota(jnp.int32, n_s.shape, 0) // heads
            key = lax.broadcasted_iota(jnp.int32, n_s.shape, 1)
            seen = (key >= b * steps) & (key <= row) & (lax.rem(me, 2 * SIDE) == 0)
            n_s = jnp.where(seen, n_s, NEG)
            m = jnp.maximum(m, jnp.max(n_s, axis=1, keepdims=True))
        p = jnp.exp2((s - m) * coef)
        total = jnp.sum(p, axis=1, keepdims=True)
        o = jnp.dot(p.astype(BF16), vt[b], preferred_element_type=F32)
        if near:
            n_p = jnp.where(seen, jnp.exp2((n_s - m) * coef), 0.0)
            total = total + jnp.sum(n_p, axis=1, keepdims=True)
            o = o + jnp.dot(n_p.astype(BF16), nl[:, :latent], preferred_element_type=F32)
        return o.astype(BF16), m * coef, total

    def pair_of(p):
        return lax.rem(y + p, SIDE)

    head_of = lax.broadcasted_iota(jnp.int32, (per, LANES), 0) & (heads - 1)
    lane_of = lax.broadcasted_iota(jnp.int32, (per, LANES), 1)
    lane = lax.broadcasted_iota(jnp.int32, (8, LANES), 1)

    def spread(column):
        one = jnp.where(head_of == lane_of, column, 0.0).reshape(steps, heads, LANES)
        return jnp.sum(one, axis=1)

    def work(p, u, near):
        b = 2 * pair_of(p) + u
        o, m, total = attend(b, near)
        ot[p, u * per : (u + 1) * per, :] = o
        tops[p, u * steps : (u + 1) * steps, :] = spread(m)
        sums[p, u * steps : (u + 1) * steps, :] = spread(total)

    owners = [(2, 0), (2, 1), (1, 0), (1, 1), (3, 0), (3, 1), (0, 1)]

    def to_owner(p, dy, dc):
        to_y = lax.rem(y + dy, SIDE)
        to_core = lax.rem(core + dc, 2)
        to = to_y * (2 * SIDE) + pair_of(p) * 2 + to_core
        k = (p * SIDE + dy) * 2 + dc
        return (
            pltpu.make_async_remote_copy(
                src_ref=st.at[p, to_core, to_y],
                dst_ref=rb.at[me],
                send_sem=r_send.at[k],
                recv_sem=r_recv.at[me],
                device_id={"ctx": to},
                device_id_type=MESH,
            ),
            pltpu.make_async_remote_copy(
                src_ref=stl.at[p, to_core],
                dst_ref=rbl.at[me],
                send_sem=r_send.at[rows + k],
                recv_sem=r_recv.at[rows + me],
                device_id={"ctx": to},
                device_id_type=MESH,
            ),
        )

    def project(pairs):
        turned = []
        for p in pairs:
            t = jnp.dot(perm[...], ot[p], preferred_element_type=F32)
            turned.append(t.astype(BF16))
            a, b = tops[p], sums[p]
            stl[p, 0] = jnp.where(lane < 16, a, pltpu.roll(b, 16, 1))
            stl[p, 1] = jnp.where(lane < 16, pltpu.roll(a, LANES - 16, 1), b)
        blocks = [[] for _ in pairs]
        for g in range(heads // 8):
            w = jnp.concatenate([vu[g * 8 + k] for k in range(8)], axis=1)
            x = jnp.concatenate([t[g * 64 : g * 64 + 64] for t in turned], axis=0)
            r = jnp.dot(x, w, preferred_element_type=F32)
            for i in range(len(pairs)):
                part = r[i * 64 : i * 64 + 64]
                blocks[i].append(
                    jnp.concatenate(
                        [part[k * 8 : k * 8 + 8, k * LANES : (k + 1) * LANES] for k in range(8)],
                        axis=1,
                    )
                )
        for i, p in enumerate(pairs):
            for c in range(2):
                half_state = jnp.concatenate(blocks[i][2 * c : 2 * c + 2], axis=0).astype(BF16)
                for k in range(SIDE):
                    st[p, c, k] = half_state[:, k * 256 : k * 256 + 256]
            mine = pair_of(p) == z

            @pl.when(mine)
            def _(p=p):
                rb[me] = st[p, core, y]
                rbl[me] = stl[p, core]

            @pl.when(jnp.logical_not(mine))
            def _(p=p):
                for copy in to_owner(p, 0, 0):
                    copy.start()

            for dy, dc in owners:
                for copy in to_owner(p, dy, dc):
                    copy.start()

    get_ku.wait()
    get_nl.wait()
    get_vu.wait()
    get_op.wait()
    absorb([y])
    for i, (dy, dz) in enumerate(across[::-1]):
        got_q(at(dy, dz))
        q_sends[19 + i].start()
    work(0, 0, True)
    work(0, 1, True)
    for dy in range(1, SIDE):
        for dz in range(SIDE):
            got_q(at(dy, dz, 1))
    absorb([pair_of(p) for p in range(1, SIDE)])
    @pl.loop(1, SIDE - 1)
    def _(p):
        work(p, 0, False)
        work(p, 1, False)

    project(range(SIDE - 1))
    work(SIDE - 1, 0, False)
    work(SIDE - 1, 1, False)
    project([SIDE - 1])

    def from_peer(source):
        return (
            pltpu.make_async_remote_copy(
                src_ref=st.at[0, 0, 0],
                dst_ref=rb.at[source],
                send_sem=r_send.at[0],
                recv_sem=r_recv.at[source],
                device_id={"ctx": sibling},
                device_id_type=MESH,
            ),
            pltpu.make_async_remote_copy(
                src_ref=stl.at[0, 0],
                dst_ref=rbl.at[source],
                send_sem=r_send.at[0],
                recv_sem=r_recv.at[rows + source],
                device_id={"ctx": sibling},
                device_id_type=MESH,
            ),
        )

    @pl.loop(0, heads * LANES // 512)
    def _(i):
        span = pl.ds(pl.multiple_of(i * 512, 512), 512)
        opt[span, :] = jnp.transpose(op[:, span])

    for copy in q_sends:
        copy.wait_send()
    for d in everyone:
        for copy in from_peer(at(*d)):
            copy.wait_recv()

    stats = rbl[...]
    top = jnp.max(stats, axis=0)
    w = jnp.exp2(stats - top[None])
    totals = pltpu.roll(stats.reshape(rows * 8, LANES), LANES - 16, 1).reshape(rows, 8, LANES)
    w = w / jnp.sum(w * totals, axis=0)[None]
    w = pltpu.roll(w.reshape(rows * 8, LANES), lax.rem(LANES - 2 * y, LANES), 1)
    acc = jnp.zeros((16, 256), F32)
    for s in range(rows):
        f = w[s * 8 : s * 8 + 8]
        f = [jnp.broadcast_to(f[:, i : i + 1], (8, LANES)) for i in (0, 1, 8, 9)]
        f = jnp.concatenate(
            [jnp.concatenate(f[:2], axis=1), jnp.concatenate(f[2:], axis=1)], axis=0
        )
        acc = acc + rb[s].astype(F32) * f
    ho[...] = acc.astype(BF16)
    hg[core, z, y] = ho[...]

    def send_h(to, source):
        return pltpu.make_async_remote_copy(
            src_ref=ho,
            dst_ref=hg.at[
                lax.rem(source, 2), lax.rem(source // 2, SIDE), source // (2 * SIDE)
            ],
            send_sem=h_send.at[to],
            recv_sem=h_recv.at[source],
            device_id={"ctx": to},
            device_id_type=MESH,
        )

    for d in everyone:
        send_h(at(*d), me).start()
    for p in range(SIDE):

        @pl.when(pair_of(p) != z)
        def _(p=p):
            for copy in to_owner(p, 0, 0):
                copy.wait_send()

        for dy, dc in owners:
            for copy in to_owner(p, dy, dc):
                copy.wait_send()
    for d in everyone:
        send_h(at(*d), at(*d)).wait_recv()

    parts = []
    for c in range(2):
        x = [[hg[c, pair, i].astype(F32) for pair in range(SIDE)] for i in range(SIDE)]
        for u in range(2):
            for i in range(SIDE):
                part = jnp.concatenate([a[u * 8 : u * 8 + 8] for a in x[i]], axis=0)
                parts.append(part.astype(BF16))
    total = jnp.dot(jnp.concatenate(parts, axis=1), opt[...], preferred_element_type=F32)
    xb[group] = total.astype(BF16)

    def send_x(to, slot):
        return pltpu.make_async_remote_copy(
            src_ref=xb.at[group],
            dst_ref=xb.at[slot],
            send_sem=x_send.at[to],
            recv_sem=x_recv.at[slot],
            device_id={"heads": to},
            device_id_type=MESH,
        )

    for i in range(1, groups):
        send_x(lax.rem(group + i, groups), group).start()
    for d in everyone:
        send_h(at(*d), me).wait_send()
    for i in range(1, groups):
        other = lax.rem(group + i, groups)
        send_x(other, other).wait_recv()
    result = xb[0].astype(F32)
    for g in range(1, groups):
        result = result + xb[g].astype(F32)
    out[...] = result.astype(out.dtype)

    for i in range(1, groups):
        send_x(lax.rem(group + i, groups), group).wait_send()


def local(groups, queries, cache, fresh, lengths, key_up, value_up, out_proj):
    cache = jnp.swapaxes(cache, 1, 2)
    out_proj = jnp.swapaxes(out_proj, 0, 1)
    heads, nope, latent = key_up.shape
    reqs, width, keys = cache.shape
    rows = fresh.shape[0]
    vdim = value_up.shape[2]
    columns = out_proj.shape[0]
    per = rows // reqs * heads
    hbm = pl.BlockSpec(memory_space=pl.ANY)
    dma = pltpu.SemaphoreType.DMA
    return pl.pallas_call(
        functools.partial(kernel, groups),
        out_shape=jax.ShapeDtypeStruct((rows, columns), BF16),
        in_specs=[hbm] * 7,
        out_specs=pl.BlockSpec(memory_space=pltpu.VMEM),
        scratch_shapes=[
            pltpu.VMEM((reqs, width, keys), BF16),
            pltpu.VMEM((reqs, keys, latent), BF16),
            pltpu.VMEM((heads, nope, latent), BF16),
            pltpu.VMEM((heads, latent, vdim), BF16),
            pltpu.VMEM((columns, heads * vdim), BF16),
            pltpu.VMEM((heads * vdim, columns), BF16),
            pltpu.VMEM((rows, width), BF16),
            pltpu.SMEM((reqs,), jnp.int32),
            pltpu.VMEM((heads, queries.shape[2]), BF16),
            pltpu.VMEM((rows, heads + heads // 2, LANES), BF16),
            pltpu.VMEM((rows, heads, width), BF16),
            pltpu.VMEM((2 * per, 2 * per), BF16),
            pltpu.VMEM((SIDE, 2 * per, latent), BF16),
            pltpu.VMEM((SIDE, 8, LANES), F32),
            pltpu.VMEM((SIDE, 8, LANES), F32),
            pltpu.VMEM((SIDE, 2, SIDE, 16, 256), BF16),
            pltpu.VMEM((SIDE, 2, 8, LANES), F32),
            pltpu.VMEM((rows, 16, 256), BF16),
            pltpu.VMEM((rows, 8, LANES), F32),
            pltpu.VMEM((16, 256), BF16),
            pltpu.VMEM((2, SIDE, SIDE, 16, 256), BF16),
            pltpu.VMEM((groups, rows, columns), BF16),
            dma((reqs,)),
            dma((6,)),
            dma((31,)),
            dma((rows,)),
            dma((2 * rows,)),
            dma((2 * rows,)),
            dma((rows,)),
            dma((rows,)),
            dma((groups,)),
            dma((groups,)),
        ],
        compiler_params=pltpu.CompilerParams(
            collective_id=0, has_side_effects=True, vmem_limit_bytes=56 * 1024 * 1024
        ),
        cost_estimate=pl.CostEstimate(
            flops=4 * 10**9, bytes_accessed=25 * 10**6, transcendentals=2 * 10**6
        ),
        name="mla_decode",
    )(queries, cache, fresh, lengths, key_up, value_up, out_proj)


def solution(mesh):
    in_specs = (
        P("ctx", "heads", None),
        P(None, "ctx", None),
        P(),
        P(),
        P("heads", None, None),
        P("heads", None, None),
        P("heads", "ctx"),
    )
    body = functools.partial(local, mesh.shape["heads"])
    return jax.shard_map(
        body, mesh=mesh, in_specs=in_specs, out_specs=P(None, "ctx"), check_vma=False
    )
```
